512 devices in a mesh: atom: 32 (over z, core), energy: 16 (over y, x).
Axes of the slice: x: 4, y: 4, z: 16, core: 2. Of those that a mesh axis runs over, the one named last changes fastest.
Arguments:
- green: bfloat16 [256, 200, 2048], P('atom', None, 'energy'), may hold values from -6 to 6
- coupling: bfloat16 [512, 800], P('atom'), may hold values from -0.625 to 0.625
- pairs: int32 [512, 2], P('atom'), may hold values from 0 to 255, as said below
- counts: int32 [32], P('atom'), may hold values from 8 to 16, as said below
- occupation: float32 [8], replicated, may hold values from 0.05 to 2
- offsets: int32 [8], replicated, may hold values from 1 to 64, as said below
Outputs:
- sigma: bfloat16 [256, 200, 2048], P('atom', None, 'energy')
The draws below stay inside these ranges and needn't reach their ends.
Inputs may be any that keep to these rules, and one draw needn't show every extreme that they name: `pairs`: slot s lies in partition p = s // 16; its first atom is one of partition p, atoms p * 8 to (p + 1) * 8 - 1. Its second atom is another atom of partition p, or one of the first 2 atoms of partition p + 1 (then its first atom is one of the last 2 atoms of partition p), or one of the last 2 atoms of partition p - 1 (then its first atom is one of the first 2 atoms of partition p); in every partition that has such a neighbour some live slot bonds to the farthest of those 2 atoms. `counts`: some partition has all its slots live. `offsets`: some mode has the largest offset.
All inputs are finite; a program needn't handle non-finite values.
Results may differ from the reference program's by a relative error of at most 0.012.
Values may be sent and summed in bfloat16 or wider, within the bound.
No kernel may reach another device: no remote copies, remote signals or barrier semaphores. Data moves between devices by JAX's collectives and lax.ppermute only.
A program may use at most 192 MiB of HBM per device.

```python
import math
import jax
import jax.numpy as jnp
from jax import lax

NORB = 10
MODES = 8
KMAX = 64
ATOM_DEV = 8
RIM = 2
PAIR_DEV = 16
PARTITIONS = 32
ATOMS = 256
PAIRS = 512
ENERGIES = 2048


def draw_pairs(key, part):
    key = jax.random.fold_in(key, 11)
    keys = jax.random.split(key, 5)
    slots = jnp.arange(PAIRS, dtype=jnp.int32)
    owner = slots // PAIR_DEV
    within = slots % PAIR_DEV
    kind = jax.random.randint(keys[1], (PAIRS,), 0, 4)
    kind = jnp.where(within == 0, 2, kind)
    kind = jnp.where(within == 1, 3, kind)
    kind = jnp.where((kind == 2) & (owner == PARTITIONS - 1), 0, kind)
    kind = jnp.where((kind == 3) & (owner == 0), 0, kind)
    free_rel = jax.random.randint(keys[0], (PAIRS,), 0, ATOM_DEV)
    rim_rel = jax.random.randint(keys[4], (PAIRS,), 0, RIM)
    first_rel = jnp.where(kind == 2, ATOM_DEV - RIM + rim_rel, jnp.where(kind == 3, rim_rel, free_rel))
    depth = jax.random.randint(keys[2], (PAIRS,), 0, RIM)
    depth = jnp.where(within < 2, RIM - 1, depth)
    step_local = jax.random.randint(keys[3], (PAIRS,), 1, ATOM_DEV)
    local_rel = (first_rel + step_local) % ATOM_DEV
    second_rel = jnp.where(kind == 2, ATOM_DEV + depth, jnp.where(kind == 3, -1 - depth, local_rel))
    base = owner * ATOM_DEV
    return jnp.stack([base + first_rel, base + second_rel], axis=1).astype(jnp.int32)


def draw_counts(key, part):
    key = jax.random.fold_in(key, 23)
    keys = jax.random.split(key, 2)
    values = jax.random.randint(keys[0], (PARTITIONS,), PAIR_DEV // 2, PAIR_DEV + 1)
    place = jax.random.randint(keys[1], (), 0, PARTITIONS)
    return values.at[place].set(PAIR_DEV).astype(jnp.int32)


def draw_offsets(key, part):
    key = jax.random.fold_in(key, 37)
    keys = jax.random.split(key, 2)
    values = jax.random.randint(keys[0], (MODES,), 1, KMAX + 1)
    place = jax.random.randint(keys[1], (), 0, MODES)
    return values.at[place].set(KMAX).astype(jnp.int32)


def block_scale(stream_key, extent, cuts, smallest, top_value):
    def one(axis_at, blocks):
        heights = jax.random.uniform(jax.random.fold_in(jax.random.fold_in(stream_key, 6), axis_at), (blocks,), jnp.float32, smallest / len(cuts), top_value / len(cuts))
        return jnp.repeat(jnp.exp(heights), extent[axis_at] // blocks).reshape((-1,) + (1,) * (len(extent) - axis_at - 1))

    loudness = one(*cuts[0])
    for cut in cuts[1:]:
        loudness = loudness * one(*cut)
    return loudness


def centred(key, extent, scale, reach, pieces=(), kind=jnp.bfloat16):
    factor_of = block_scale(key, extent, pieces, -0.22, 0.18) if pieces else 1.0
    drawn = jax.random.normal(key, extent, jnp.float32) * scale * factor_of
    return jnp.minimum(jnp.maximum(drawn, -reach), reach).astype(kind)


def setup_inputs(seed: int = 0) -> dict:
    streams_of = jax.random.split(jax.random.key(seed), 7)
    return {
        "green": centred(streams_of[0], (ATOMS, 2 * NORB * NORB, ENERGIES), 1.0, 6.0, ((0, 32), (2, 16))),
        "coupling": centred(streams_of[1], (PAIRS, MODES * NORB * NORB), (8 * NORB) ** -0.5, 0.625, ((0, 32),)),
        "pairs": draw_pairs(jax.random.fold_in(streams_of[6], 71), 0),
        "counts": draw_counts(jax.random.fold_in(streams_of[6], 71), 0),
        "occupation": jnp.clip(jnp.exp(jax.random.uniform(streams_of[4], (MODES,), jnp.float32, math.log(0.05), math.log(2.0))), 0.05, 2.0),
        "offsets": draw_offsets(jax.random.fold_in(streams_of[6], 71), 0),
    }


def sandwich(blocks, weights, transpose):
    if transpose:
        inner = jnp.einsum("pji,prjke->prike", weights, blocks, precision=lax.Precision.HIGHEST)
        return jnp.einsum("prike,pkl->prile", inner, weights, precision=lax.Precision.HIGHEST)
    inner = jnp.einsum("pij,prjke->prike", weights, blocks, precision=lax.Precision.HIGHEST)
    return jnp.einsum("prike,plk->prile", inner, weights, precision=lax.Precision.HIGHEST)


def reference(green, coupling, pairs, counts, occupation, offsets):
    slab = 2 * NORB * NORB
    padded = jnp.pad(green, ((0, 0), (0, 0), (KMAX, KMAX)))
    slots = jnp.arange(PAIRS, dtype=jnp.int32)
    live = ((slots % PAIR_DEV) < counts[slots // PAIR_DEV]).astype(jnp.float32)
    block = math.gcd(PAIRS, 64)
    steps_count = PAIRS // block
    first_all = pairs[:, 0].reshape(steps_count, block)
    second_all = pairs[:, 1].reshape(steps_count, block)
    live_all = live.reshape(steps_count, block)
    coup_all = coupling.reshape(steps_count, block, MODES, NORB, NORB)

    def shifted_rows(rows, occ, step_size):
        lower = lax.dynamic_slice_in_dim(rows, (KMAX - step_size).astype(jnp.int32), ENERGIES, 2).astype(jnp.float32)
        upper = lax.dynamic_slice_in_dim(rows, (KMAX + step_size).astype(jnp.int32), ENERGIES, 2).astype(jnp.float32)
        mixed = (occ * lower + (occ + 1.0) * upper).astype(jnp.bfloat16)
        return mixed.astype(jnp.float32).reshape(block, 2, NORB, NORB, ENERGIES)

    def visit(total, items):
        first, second, mask, coup = items
        rows_a = padded[first]
        rows_b = padded[second]
        for mode in range(MODES):
            occ = occupation[mode]
            step_size = offsets[mode]
            weights = coup[:, mode].astype(jnp.float32)
            part_a = shifted_rows(rows_a, occ, step_size)
            part_b = shifted_rows(rows_b, occ, step_size)
            to_a = sandwich(part_b, weights, False) * mask[:, None, None, None, None]
            to_b = sandwich(part_a, weights, True) * mask[:, None, None, None, None]
            total = total.at[first].add(to_a.reshape(block, slab, ENERGIES))
            total = total.at[second].add(to_b.reshape(block, slab, ENERGIES))
        return total, None

    total = jnp.zeros((ATOMS, slab, ENERGIES), jnp.float32)
    total, _ = lax.scan(visit, total, (first_all, second_all, live_all, coup_all))
    return total.astype(jnp.bfloat16)
```

```python
import functools

import jax
import jax.numpy as jnp
from jax import lax
from jax.experimental import pallas as pl
from jax.experimental.pallas import tpu as pltpu
from jax.sharding import PartitionSpec as P

NORB = 10
MODES = 8
KMAX = 64
SQ = NORB * NORB
ROWS = 104
LANES = 128
DEPTH = MODES * LANES
BF = jnp.bfloat16
F32 = jnp.float32
VMEM = pl.BlockSpec(memory_space=pltpu.VMEM)
SMEM = pl.BlockSpec(memory_space=pltpu.SMEM)


def iota(shape, dim):
    return lax.broadcasted_iota(jnp.int32, shape, dim)


def build_kernel(occ_ref, off_ref, cnt_ref, coup_ref, t_ref, tt_ref, s_ref, cm, v, c12):
    slots = coup_ref.shape[0]
    coup = coup_ref[...].astype(F32)
    width = 7 * LANES
    coup = jnp.concatenate([coup, jnp.zeros((slots, width - MODES * SQ), F32)], axis=1)
    lane = iota((slots, LANES), 1)
    for m in range(MODES):
        part = coup if m == 0 else pltpu.roll(coup, width - m * SQ, 1)
        cm[m * slots : (m + 1) * slots, :] = jnp.where(lane < SQ, part[:, :LANES], 0.0)

    ij = iota((LANES, LANES), 0)
    jk = iota((LANES, LANES), 1)
    valid = (ij < SQ) & (jk < SQ)
    i_of, j_of = ij // NORB, ij % NORB
    j_to, k_to = jk // NORB, jk % NORB
    row = iota((16, LANES), 0) % NORB
    col = iota((16, LANES), 1)
    sub = iota((8, LANES), 0)

    def expand(masked, keep, other, out_ref):
        spread = jnp.concatenate(
            [
                jnp.where(valid & (other == j_to), 1.0, 0.0),
                jnp.where(valid & (other == k_to), 1.0, 0.0),
            ],
            axis=1,
        ).astype(BF)
        keep = jnp.where(keep == row, 1.0, 0.0)

        def fill(s, carry):
            for m in range(MODES):
                line = cm[pl.ds(m * slots + s, 1), :]
                v[pl.ds(pl.multiple_of(s * (16 * MODES) + m * 16, 16), 16), :] = (
                    jnp.broadcast_to(line, (16, LANES)) * keep
                ).astype(BF)
            return carry

        lax.fori_loop(0, cnt_ref[0], fill, 0)
        for part in range(slots // 2):
            at = part * 32 * MODES
            c12[at : at + 32 * MODES, :] = jnp.dot(
                v[at : at + 32 * MODES, :], spread, preferred_element_type=F32
            )

        def product(s, carry):
            for m in range(MODES):
                base = pl.multiple_of(s * (16 * MODES) + m * 16, 16)
                first = c12[pl.ds(base, 16), :LANES]
                second = c12[pl.ds(base, 16), LANES:]
                turns = [
                    second[0:8],
                    second[8:16],
                    pltpu.roll(second, 10, 0)[0:8],
                    pltpu.roll(second, 12, 0)[0:8],
                    pltpu.roll(second, 14, 0)[0:8],
                ]
                spreads = [jnp.broadcast_to(first[i : i + 1], (8, LANES)) for i in range(NORB)]
                rows = []
                for g in range(ROWS // 8):
                    lo = 8 * g // NORB
                    hi = min((8 * g + 7) // NORB, NORB - 1)
                    left = spreads[lo]
                    if hi != lo:
                        left = jnp.where(sub < NORB * hi - 8 * g, left, spreads[hi])
                    rows.append(left * turns[g % 5])
                out_ref[s, :, m * LANES : (m + 1) * LANES] = jnp.concatenate(rows, axis=0).astype(BF)
            return carry

        lax.fori_loop(0, cnt_ref[0], product, 0)

    v[...] = jnp.zeros(v.shape, BF)
    expand(cm, col // NORB, j_of, t_ref)
    expand(cm, col % NORB, i_of, tt_ref)

    e_in = iota((2 * LANES, LANES), 0)
    e_out = iota((2 * LANES, LANES), 1)
    low = jnp.where(e_in < 128, e_in, jnp.where(e_in < 192, e_in - 192, e_in - 64))
    high = jnp.where(e_in < 128, e_in, jnp.where(e_in < 192, e_in, e_in - 256))
    for m in range(MODES):
        occ = occ_ref[m]
        step = off_ref[m]
        for which, e_of in enumerate((low, high)):
            s_ref[which, :, m * LANES : (m + 1) * LANES] = jnp.where(
                e_of == e_out - step, occ, jnp.where(e_of == e_out + step, occ + 1.0, 0.0)
            ).astype(BF)


def shift_atom(center, halo, s_ref, which, gf, store):
    gf[0:200, :LANES] = center.astype(F32)
    gf[0:200, LANES:] = halo.astype(F32)
    lhs = jnp.concatenate([gf[0:104, :], gf[100:204, :]], axis=0).astype(BF)
    for t in range(MODES // 2):
        out = jnp.dot(lhs, s_ref[which, :, t * 256 : (t + 1) * 256], preferred_element_type=F32)
        for mm in range(2):
            for r in range(2):
                store(
                    2 * t + mm,
                    r,
                    out[r * ROWS : (r + 1) * ROWS, mm * LANES : (mm + 1) * LANES].astype(BF),
                )


def halo_of(fr_ref, fl_ref, x):
    left = iota((200, LANES), 1) < 64
    a = fr_ref[x % 4]
    b = fl_ref[x % 4]
    return jnp.where(left, a, b) if x < 4 else jnp.where(left, b, a)


def prepare(x_ref, gf, count):
    gf[200:208, :] = jnp.zeros((8, 256), F32)
    for x in range(count):
        for m in range(MODES):
            x_ref[x, m * LANES + 96 : (m + 1) * LANES, :] = jnp.zeros((32, 256), BF)


def store_in(x_ref, at):
    def store(m, r, value):
        x_ref[at, m * LANES : m * LANES + ROWS, r * LANES : (r + 1) * LANES] = value

    return store


def pack_rows(total, gf):
    gf[0:ROWS, :LANES] = total[:, :LANES]
    gf[SQ : SQ + ROWS, :LANES] = total[:, LANES:]
    return gf[0:200, :LANES].astype(BF)


def rim_kernel(
    cnt_ref, fst_ref, snd_ref, odd_ref, g_ref, fr_ref, fl_ref, s_ref, tt_ref, cross_ref, near_ref, x, part, gf
):
    prepare(x, gf, 4)
    rims = (0, 1, 6, 7)
    halos = []
    for at, atom in enumerate(rims):
        halo = halo_of(fr_ref, fl_ref, atom)
        halos.append(halo)
        shift_atom(g_ref[atom], halo, s_ref, atom // 4, gf, store_in(x, at))
    part[...] = jnp.zeros(part.shape, F32)

    def visit(s, carry):
        second = snd_ref[s]
        first = fst_ref[s]

        @pl.when((second < 0) | (second >= 8))
        def _():
            to = jnp.where(second < 0, second + 2, second - 6)
            of = jnp.where(first >= 4, first - 4, first)
            part[to] = part[to] + jnp.dot(tt_ref[s], x[of], preferred_element_type=F32)

        return carry

    lax.fori_loop(0, cnt_ref[0], visit, 0)
    odd = odd_ref[0]

    def fill(ref, side):
        for j in range(2):
            ref[j] = g_ref[6 * side + j]
            ref[2 + j] = halos[2 * side + j]
            ref[4 + j] = pack_rows(part[2 * side + j], gf)

    @pl.when(odd == 1)
    def _():
        fill(cross_ref, 1)
        fill(near_ref, 0)

    @pl.when(odd == 0)
    def _():
        fill(cross_ref, 0)
        fill(near_ref, 1)


def local_kernel(cnt_ref, fst_ref, snd_ref, g_ref, fr_ref, fl_ref, s_ref, t_ref, tt_ref, acc, x, gf):
    prepare(x, gf, 8)
    for atom in range(8):
        shift_atom(g_ref[atom], halo_of(fr_ref, fl_ref, atom), s_ref, atom // 4, gf, store_in(x, atom))
    acc[...] = jnp.zeros(acc.shape, F32)

    def visit(s, carry):
        second = snd_ref[s]
        first = fst_ref[s]

        @pl.when((second >= 0) & (second < 8))
        def _():
            acc[first] = acc[first] + jnp.dot(t_ref[s], x[second], preferred_element_type=F32)
            acc[second] = acc[second] + jnp.dot(tt_ref[s], x[first], preferred_element_type=F32)

        return carry

    lax.fori_loop(0, cnt_ref[0], visit, 0)


def final_kernel(
    cnt_ref, fst_ref, snd_ref, odd_ref, cross_ref, near_ref, s_ref, t_ref, acc_ref, out_ref, x, acc, gf
):
    prepare(x, gf, 4)
    odd = odd_ref[0]

    def take(ref, side):
        for j in range(2):
            shift_atom(ref[j], ref[2 + j], s_ref, 1 - side, gf, store_in(x, 2 * side + j))

    @pl.when(odd == 1)
    def _():
        take(cross_ref, 1)
        take(near_ref, 0)

    @pl.when(odd == 0)
    def _():
        take(cross_ref, 0)
        take(near_ref, 1)

    acc[...] = acc_ref[...]

    def visit(s, carry):
        second = snd_ref[s]
        first = fst_ref[s]

        @pl.when((second < 0) | (second >= 8))
        def _():
            of = jnp.where(second < 0, second + 2, second - 6)
            acc[first] = acc[first] + jnp.dot(t_ref[s], x[of], preferred_element_type=F32)

        return carry

    lax.fori_loop(0, cnt_ref[0], visit, 0)
    for atom in range(8):
        gf[0:ROWS, :LANES] = acc[atom, :, :LANES]
        gf[SQ : SQ + ROWS, :LANES] = acc[atom, :, LANES:]
        total = gf[0:200, :LANES]
        if atom in (0, 1, 6, 7):
            side = atom // 4
            j = atom - 6 * side
            got = jnp.where(odd == side, cross_ref[4 + j].astype(F32), near_ref[4 + j].astype(F32))
            total = total + got
        out_ref[atom] = total.astype(BF)


def swap(value, axis, start):
    count = lax.axis_size(axis)
    pairs = [(i, i + 1) for i in range(start, count - 1, 2)]
    return lax.ppermute(value, axis, pairs + [(b, a) for a, b in pairs])


def step_of(value, axis, by):
    count = lax.axis_size(axis)
    return lax.ppermute(value, axis, [(i, i + by) for i in range(count) if 0 <= i + by < count])


def call(kernel, outs, scratch, flops, moved, specs):
    return pl.pallas_call(
        kernel,
        out_shape=outs,
        in_specs=specs,
        out_specs=jax.tree.map(lambda _: VMEM, outs),
        scratch_shapes=scratch,
        compiler_params=pltpu.CompilerParams(vmem_limit_bytes=40 * 1024 * 1024),
        cost_estimate=pl.CostEstimate(flops=flops, bytes_accessed=moved, transcendentals=0),
    )


def per_device(green, coupling, pairs, counts, occupation, offsets):
    atoms, slab, e_dev = green.shape
    slots = pairs.shape[0]
    part = lax.axis_index("atom")
    rel = pairs - part * atoms
    first, second = rel[:, 0], rel[:, 1]
    odd = jnp.reshape(part % 2, (1,)).astype(jnp.int32)
    half = atoms // 2
    to_right = jnp.concatenate([green[:half, :, KMAX:], green[half:, :, KMAX:]], axis=2)
    to_left = jnp.concatenate([green[half:, :, :KMAX], green[:half, :, :KMAX]], axis=2)
    fr = step_of(to_right, "energy", 1)
    fl = step_of(to_left, "energy", -1)

    shape = jax.ShapeDtypeStruct
    tens = shape((slots, ROWS, DEPTH), BF)
    gf = pltpu.VMEM((208, 256), F32)
    t, tt, s = call(
        build_kernel,
        (tens, tens, shape((2, 256, DEPTH), BF)),
        [
            pltpu.VMEM((MODES * slots, LANES), F32),
            pltpu.VMEM((MODES * slots * 16, LANES), BF),
            pltpu.VMEM((MODES * slots * 16, 256), F32),
        ],
        int(3e9),
        int(8e6),
        [SMEM, SMEM, SMEM, VMEM],
    )(occupation, offsets, counts, coupling)

    payload = shape((6, slab, e_dev), BF)
    cross, near = call(
        rim_kernel,
        (payload, payload),
        [pltpu.VMEM((4, DEPTH, 256), BF), pltpu.VMEM((4, ROWS, 256), F32), gf],
        int(1e9),
        int(1e6),
        [SMEM] * 4 + [VMEM] * 5,
    )(counts, first, second, odd, green, fr, fl, s, tt)
    cross = swap(cross, "atom", 1)
    near = swap(near, "atom", 0)

    acc = call(
        local_kernel,
        shape((atoms, ROWS, 256), F32),
        [pltpu.VMEM((8, DEPTH, 256), BF), gf],
        int(3e9),
        int(1e6),
        [SMEM] * 3 + [VMEM] * 6,
    )(counts, first, second, green, fr, fl, s, t, tt)

    return call(
        final_kernel,
        shape((atoms, slab, e_dev), BF),
        [pltpu.VMEM((4, DEPTH, 256), BF), pltpu.VMEM((atoms, ROWS, 256), F32), gf],
        int(1e9),
        int(1e6),
        [SMEM] * 4 + [VMEM] * 5,
    )(counts, first, second, odd, cross, near, s, t, acc)


def solution(mesh):
    placed = (P("atom", None, "energy"), P("atom", None), P("atom", None), P("atom"), P(), P())
    return jax.shard_map(
        per_device, mesh=mesh, in_specs=placed, out_specs=P("atom", None, "energy"), check_vma=False
    )
```

```python
import jax
import jax.numpy as jnp
from jax import lax
from jax.experimental import pallas as pl
from jax.experimental.pallas import tpu as pltpu
from jax.sharding import PartitionSpec as P

NORB = 10
MODES = 8
KMAX = 64
SQ = NORB * NORB
ROWS = 104
PITCH = 112
LANES = 128
DEPTH = MODES * LANES
SLOTS = 16
ATOMS = 8
SLAB = 2 * SQ
LISTS = 48
BF = jnp.bfloat16
F32 = jnp.float32
I32 = jnp.int32
VMEM = pl.BlockSpec(memory_space=pltpu.VMEM)
SMEM = pl.BlockSpec(memory_space=pltpu.SMEM)
HBM = pl.BlockSpec(memory_space=pltpu.HBM)


def iota(shape, dim):
    return lax.broadcasted_iota(I32, shape, dim)


def pack_kernel(
    g_ref, coup_ref, pairs_hbm, occ_hbm, off_hbm, to_a, to_b, g, coup, ints, occ, pairs_ref, off_ref, sems
):
    moves = (
        (g_ref, g),
        (pairs_hbm, pairs_ref),
        (occ_hbm, occ),
        (off_hbm, off_ref),
        (coup_ref, coup),
    )
    copies = [pltpu.make_async_copy(src, dst, sems.at[i]) for i, (src, dst) in enumerate(moves)]
    for copy in copies:
        copy.start()
    for copy in copies[1:4]:
        copy.wait()
    base = lax.axis_index("atom") * ATOMS
    for s in range(SLOTS):
        ints[s] = pairs_ref[0, s] - base
        ints[SLOTS + s] = pairs_ref[1, s] - base
    for m in range(MODES):
        ints[2 * SLOTS + m] = off_ref[m]
    odd = lax.axis_index("energy") % 2
    half = ATOMS // 2
    low = jnp.where(odd == 0, 1, 0)
    pick = (iota((SLAB, LANES), 1) // KMAX) == odd
    copies[0].wait()
    for x in range(half):
        turned = pltpu.roll(g[x + half * odd].astype(F32), KMAX, 1)
        kept = g[x + half * low].astype(F32)
        to_a[x] = jnp.where(pick, turned, kept).astype(BF)
        to_b[x] = jnp.where(pick, kept, turned).astype(BF)
    copies[4].wait()


def build_kernel(cnt_ref, occ_ref, ints_ref, coup_ref, t_ref, s_ref, jobs_ref, cm, v, c12):
    count = cnt_ref[0]

    def listed(s, carry):
        near, far = carry
        first = ints_ref[s]
        second = ints_ref[SLOTS + s]
        local = jnp.where((second >= 0) & (second < ATOMS), 1, 0)
        rim = jnp.where(first >= 4, first - 4, first)
        out = jnp.where(second < 0, second + 2, second - 6)
        jobs_ref[near] = s + 64 * second + 4096 * first
        jobs_ref[near + 1] = s + SLOTS + 64 * first + 4096 * second
        jobs_ref[LISTS + far] = s + SLOTS + 64 * rim + 4096 * out
        jobs_ref[2 * LISTS + far] = s + 64 * out + 4096 * rim
        return near + 2 * local, far + 1 - local

    near, far = lax.fori_loop(0, count, listed, (jnp.int32(0), jnp.int32(0)))
    for j in range(8):
        jobs_ref[near + j] = 4096 * ATOMS
        jobs_ref[LISTS + far + j] = 4096 * 4
        jobs_ref[2 * LISTS + far + j] = 4096 * 4
    jobs_ref[3 * LISTS] = near
    jobs_ref[3 * LISTS + 1] = far

    coup = coup_ref[...].astype(F32)
    width = 7 * LANES
    coup = jnp.concatenate([coup, jnp.zeros((SLOTS, width - MODES * SQ), F32)], axis=1)
    lane = iota((SLOTS, LANES), 1)
    for m in range(MODES):
        part = coup if m == 0 else pltpu.roll(coup, width - m * SQ, 1)
        cm[m * SLOTS : (m + 1) * SLOTS, :] = jnp.where(lane < SQ, part[:, :LANES], 0.0)

    ij = iota((LANES, LANES), 0)
    jk = iota((LANES, LANES), 1)
    valid = (ij < SQ) & (jk < SQ)
    row = iota((16, LANES), 0) % NORB
    col = iota((16, LANES), 1)
    sub = iota((8, LANES), 0)

    def expand(keep, other, at):
        spread = jnp.concatenate(
            [
                jnp.where(valid & (other == jk // NORB), 1.0, 0.0),
                jnp.where(valid & (other == jk % NORB), 1.0, 0.0),
            ],
            axis=1,
        ).astype(BF)
        keep = jnp.where(keep == row, 1.0, 0.0)

        def fill(s, carry):
            for m in range(MODES):
                line = cm[pl.ds(m * SLOTS + s, 1), :]
                v[pl.ds(pl.multiple_of(s * (16 * MODES) + m * 16, 16), 16), :] = (
                    jnp.broadcast_to(line, (16, LANES)) * keep
                ).astype(BF)
            return carry

        lax.fori_loop(0, count, fill, 0)
        for part in range(SLOTS // 2):
            lo = part * 32 * MODES
            c12[lo : lo + 32 * MODES, :] = jnp.dot(
                v[lo : lo + 32 * MODES, :], spread, preferred_element_type=F32
            )

        def product(s, carry):
            for m in range(MODES):
                base = pl.multiple_of(s * (16 * MODES) + m * 16, 16)
                first = c12[pl.ds(base, 16), :LANES]
                second = c12[pl.ds(base, 16), LANES:]
                turns = [
                    second[0:8],
                    second[8:16],
                    pltpu.roll(second, 10, 0)[0:8],
                    pltpu.roll(second, 12, 0)[0:8],
                    pltpu.roll(second, 14, 0)[0:8],
                ]
                spreads = [jnp.broadcast_to(first[i : i + 1], (8, LANES)) for i in range(NORB)]
                rows = []
                for g in range(ROWS // 8):
                    lo = 8 * g // NORB
                    hi = min((8 * g + 7) // NORB, NORB - 1)
                    left = spreads[lo]
                    if hi != lo:
                        left = jnp.where(sub < NORB * hi - 8 * g, left, spreads[hi])
                    rows.append(left * turns[g % 5])
                t_ref[at + s, :, m * LANES : (m + 1) * LANES] = jnp.concatenate(rows, axis=0).astype(BF)
            return carry

        lax.fori_loop(0, count, product, 0)

    expand(col // NORB, ij % NORB, 0)
    expand(col % NORB, ij // NORB, SLOTS)

    odd = lax.axis_index("energy") % 2
    e_in = iota((2 * LANES, LANES), 0)
    e_out = iota((2 * LANES, LANES), 1)
    left_first = jnp.where(e_in < 128, e_in, jnp.where(e_in < 192, e_in - 192, e_in - 64))
    right_first = jnp.where(e_in < 128, e_in, jnp.where(e_in < 192, e_in, e_in - 256))
    orders = (jnp.where(odd == 1, left_first, right_first), jnp.where(odd == 1, right_first, left_first))
    for m in range(MODES):
        occ = occ_ref[m]
        step = ints_ref[2 * SLOTS + m]
        for which in range(2):
            away = orders[which] - e_out
            s_ref[which, :, m * LANES : (m + 1) * LANES] = jnp.where(
                away == -step, occ, jnp.where(away == step, occ + 1.0, 0.0)
            ).astype(BF)


def shift_atom(center, halo, s_ref, which, lhs, low, store):
    lhs[0:ROWS, :LANES] = center[0:ROWS]
    lhs[0:ROWS, LANES:] = halo[0:ROWS]
    low[0:ROWS, :LANES] = center[96:SLAB].astype(F32)
    low[0:ROWS, LANES:] = halo[96:SLAB].astype(F32)
    lhs[PITCH : PITCH + ROWS, :] = low[4 : 4 + ROWS, :].astype(BF)
    for t in range(MODES // 2):
        out = jnp.dot(lhs[...], s_ref[which, :, t * 256 : (t + 1) * 256], preferred_element_type=F32)
        for mm in range(2):
            for r in range(2):
                store(
                    2 * t + mm,
                    r,
                    out[r * PITCH : r * PITCH + ROWS, mm * LANES : (mm + 1) * LANES].astype(BF),
                )


def halo_of(from_a, from_b, x):
    left = iota((SLAB, LANES), 1) < KMAX
    a = from_a[x % 4]
    b = from_b[x % 4]
    return jnp.where(left, a, b) if x < 4 else jnp.where(left, b, a)


def prepare(x_ref, lhs, low, count):
    low[:, ROWS:, :] = jnp.zeros((low.shape[0], 8, 256), F32)
    lhs[:, 96:PITCH, :] = jnp.zeros((lhs.shape[0], 16, 256), BF)
    lhs[:, PITCH + 96 :, :] = jnp.zeros((lhs.shape[0], 16, 256), BF)
    for x in range(count):
        for m in range(MODES):
            x_ref[x, m * LANES + 96 : (m + 1) * LANES, :] = jnp.zeros((32, 256), BF)


def store_in(x_ref, at):
    def store(m, r, value):
        x_ref[at, m * LANES : m * LANES + ROWS, r * LANES : (r + 1) * LANES] = value

    return store


def unfold(total, rows):
    rows[0:ROWS, :] = total[:, :LANES]
    rows[SQ : SQ + ROWS, :] = total[:, LANES:]
    return rows[0:SLAB, :]


def run_jobs(jobs_ref, at, count, chunk, t_ref, x_ref, acc):
    def step(i, carry):
        for j in range(chunk):
            job = jobs_ref[at + i * chunk + j]
            t, src, dst = job & 63, (job >> 6) & 63, job >> 12
            acc[dst] = acc[dst] + jnp.dot(t_ref[t], x_ref[src], preferred_element_type=F32)
        return carry

    lax.fori_loop(0, (count + chunk - 1) // chunk, step, 0)


def rim_kernel(jobs_ref, g_ref, from_a, from_b, s_ref, t_ref, cross_ref, near_ref, x, part, lhs, low, rows):
    prepare(x, lhs, low, 4)
    halos = []
    for at, atom in enumerate((0, 1, 6, 7)):
        halo = halo_of(from_a, from_b, atom)
        halos.append(halo)
        shift_atom(g_ref[atom], halo, s_ref, atom // 4, lhs.at[at], low.at[at], store_in(x, at))
    part[...] = jnp.zeros(part.shape, F32)
    run_jobs(jobs_ref, LISTS, jobs_ref[3 * LISTS + 1], 4, t_ref, x, part)
    odd = lax.axis_index("atom") % 2

    def fill(ref, side):
        for j in range(2):
            ref[j] = g_ref[6 * side + j]
            ref[2 + j] = halos[2 * side + j]
            ref[4 + j] = unfold(part[2 * side + j], rows).astype(BF)

    @pl.when(odd == 1)
    def _():
        fill(cross_ref, 1)
        fill(near_ref, 0)

    @pl.when(odd == 0)
    def _():
        fill(cross_ref, 0)
        fill(near_ref, 1)


def local_kernel(jobs_ref, g_ref, from_a, from_b, s_ref, t_ref, inner_ref, rim_ref, x, acc, lhs, low, rows):
    prepare(x, lhs, low, ATOMS)
    for atom in range(ATOMS):
        halo = halo_of(from_a, from_b, atom)
        shift_atom(g_ref[atom], halo, s_ref, atom // 4, lhs.at[atom], low.at[atom], store_in(x, atom))
    acc[...] = jnp.zeros(acc.shape, F32)
    run_jobs(jobs_ref, 0, jobs_ref[3 * LISTS], 8, t_ref, x, acc)
    for j in range(4):
        inner_ref[j] = unfold(acc[2 + j], rows).astype(BF)
        rim_ref[j] = acc[j if j < 2 else j + 4]


def final_kernel(
    jobs_ref, cross_ref, near_ref, s_ref, t_ref, inner_ref, rim_ref, out_ref, x, acc, done, lhs, low, rows, sems
):
    early = pltpu.make_async_copy(inner_ref, out_ref.at[2:6], sems.at[0])
    early.start()
    prepare(x, lhs, low, 4)
    odd = lax.axis_index("atom") % 2

    def take(ref, side):
        for j in range(2):
            at = 2 * side + j
            shift_atom(ref[j], ref[2 + j], s_ref, 1 - side, lhs.at[at], low.at[at], store_in(x, at))

    @pl.when(odd == 1)
    def _():
        take(cross_ref, 1)
        take(near_ref, 0)

    @pl.when(odd == 0)
    def _():
        take(cross_ref, 0)
        take(near_ref, 1)

    acc[0:4] = rim_ref[...]
    run_jobs(jobs_ref, 2 * LISTS, jobs_ref[3 * LISTS + 1], 4, t_ref, x, acc)
    for j in range(4):
        side = j // 2
        got = jnp.where(
            odd == side, cross_ref[4 + j % 2].astype(F32), near_ref[4 + j % 2].astype(F32)
        )
        done[j] = (unfold(acc[j], rows) + got).astype(BF)
    lower = pltpu.make_async_copy(done.at[0:2], out_ref.at[0:2], sems.at[1])
    upper = pltpu.make_async_copy(done.at[2:4], out_ref.at[6:8], sems.at[2])
    lower.start()
    upper.start()
    early.wait()
    lower.wait()
    upper.wait()


def swap(value, axis, start):
    count = lax.axis_size(axis)
    pairs = [(i, i + 1) for i in range(start, count - 1, 2)]
    return lax.ppermute(value, axis, pairs + [(b, a) for a, b in pairs])


def call(kernel, outs, scratch, flops, moved, specs, out_specs, grant=40):
    return pl.pallas_call(
        kernel,
        out_shape=outs,
        in_specs=specs,
        out_specs=out_specs,
        scratch_shapes=scratch,
        compiler_params=pltpu.CompilerParams(vmem_limit_bytes=grant * 1024 * 1024),
        cost_estimate=pl.CostEstimate(flops=flops, bytes_accessed=moved, transcendentals=0),
    )


def per_device(green, coupling, pairs, counts, occupation, offsets):
    atoms, slab, e_dev = green.shape
    shape = jax.ShapeDtypeStruct
    dma = pltpu.SemaphoreType.DMA

    half = shape((atoms // 2, slab, e_dev), BF)
    to_a, to_b, g, coup, ints, occ = call(
        pack_kernel,
        (half, half, shape(green.shape, BF), shape(coupling.shape, BF), shape((2 * SLOTS + MODES,), I32), shape((MODES,), F32)),
        [
            pltpu.SMEM((2, SLOTS), I32),
            pltpu.SMEM((MODES,), I32),
            dma((5,)),
        ],
        int(1e6),
        int(1e6),
        [HBM] * 5,
        (VMEM, VMEM, VMEM, VMEM, SMEM, SMEM),
    )(*[pltpu.with_memory_space_constraint(v, pltpu.HBM) for v in (green, coupling, pairs.T, occupation, offsets)])
    from_b = swap(to_b, "energy", 1)
    from_a = swap(to_a, "energy", 0)

    t, s, jobs = call(
        build_kernel,
        (shape((2 * SLOTS, ROWS, DEPTH), BF), shape((2, 256, DEPTH), BF), shape((3 * LISTS + 8,), I32)),
        [
            pltpu.VMEM((MODES * SLOTS, LANES), F32),
            pltpu.VMEM((MODES * SLOTS * 16, LANES), BF),
            pltpu.VMEM((MODES * SLOTS * 16, 256), F32),
        ],
        int(3e9),
        int(8e6),
        [SMEM, SMEM, SMEM, VMEM],
        (VMEM, VMEM, SMEM),
    )(counts, occ, ints, coup)

    def scratch(count, sums):
        return [
            pltpu.VMEM((count, DEPTH, 256), BF),
            pltpu.VMEM((sums, ROWS, 256), F32),
        ], [
            pltpu.VMEM((count, 2 * PITCH, 256), BF),
            pltpu.VMEM((count, PITCH, 256), F32),
            pltpu.VMEM((208, LANES), F32),
        ]

    payload = shape((6, slab, e_dev), BF)
    main, spare = scratch(4, 5)
    cross, near = call(
        rim_kernel, (payload, payload), main + spare, int(1e9), int(1e6), [SMEM] + [VMEM] * 5, (VMEM, VMEM)
    )(jobs, g, from_a, from_b, s, t)
    cross = swap(cross, "atom", 1)
    near = swap(near, "atom", 0)

    main, spare = scratch(8, 9)
    inner, rim = call(
        local_kernel,
        (shape((4, slab, e_dev), BF), shape((4, ROWS, 256), F32)),
        main + spare,
        int(3e9),
        int(1e6),
        [SMEM] + [VMEM] * 5,
        (VMEM, VMEM),
    )(jobs, g, from_a, from_b, s, t)

    main, spare = scratch(4, 5)
    return call(
        final_kernel,
        shape((atoms, slab, e_dev), BF),
        main + [pltpu.VMEM((4, slab, e_dev), BF)] + spare + [dma((3,))],
        int(1e9),
        int(1e6),
        [SMEM] + [VMEM] * 6,
        HBM,
    )(jobs, cross, near, s, t, inner, rim)


def solution(mesh):
    placed = (P("atom", None, "energy"), P("atom", None), P("atom", None), P("atom"), P(), P())
    return jax.shard_map(
        per_device, mesh=mesh, in_specs=placed, out_specs=P("atom", None, "energy"), check_vma=False
    )
```

```python
import jax
import jax.numpy as jnp
from jax import lax
from jax.experimental import pallas as pl
from jax.experimental.pallas import tpu as pltpu
from jax.sharding import PartitionSpec as P

NORB = 10
MODES = 8
KMAX = 64
SQ = NORB * NORB
ROWS = 104
PITCH = 112
LANES = 128
DEPTH = MODES * LANES
SLOTS = 16
ATOMS = 8
SLAB = 2 * SQ
LISTS = 48
BF = jnp.bfloat16
F32 = jnp.float32
I32 = jnp.int32
VMEM = pl.BlockSpec(memory_space=pltpu.VMEM)
SMEM = pl.BlockSpec(memory_space=pltpu.SMEM)
HBM = pl.BlockSpec(memory_space=pltpu.HBM)


def iota(shape, dim):
    return lax.broadcasted_iota(I32, shape, dim)


def pack_kernel(g_hbm, coup_hbm, pairs_hbm, occ_hbm, off_hbm, to_a, to_b, g, coup, pairs, occ, off, sems):
    half = ATOMS // 2
    moves = ((g_hbm, g), (coup_hbm, coup), (pairs_hbm, pairs), (occ_hbm, occ), (off_hbm, off))
    copies = [pltpu.make_async_copy(src, dst, sems.at[i]) for i, (src, dst) in enumerate(moves)]
    for copy in copies:
        copy.start()
    odd = lax.axis_index("energy") % 2
    pick = (iota((SLAB, LANES), 1) // KMAX) == odd
    copies[0].wait()
    for x in range(half):
        turned = pltpu.roll(g[x + half * odd].astype(F32), KMAX, 1).astype(BF)
        kept = g[x + half - half * odd]
        to_a[x] = jnp.where(pick, turned, kept)
        to_b[x] = jnp.where(pick, kept, turned)
    for copy in copies[1:]:
        copy.wait()


def build_kernel(cnt_ref, pairs_ref, occ_ref, off_ref, coup_ref, t_ref, s_ref, jobs_ref, x_ref, cm, v, c12):
    count = cnt_ref[0]
    base = lax.axis_index("atom") * ATOMS
    for x in range(ATOMS):
        for m in range(MODES):
            x_ref[x, m * LANES + 96 : (m + 1) * LANES, :] = jnp.zeros((32, 256), BF)

    def listed(s, carry):
        near, far = carry
        first = pairs_ref[0, s] - base
        second = pairs_ref[1, s] - base
        local = jnp.where((second >= 0) & (second < ATOMS), 1, 0)
        rim = jnp.where(first >= 4, first - 4, first)
        out = jnp.where(second < 0, second + 2, second - 6)
        jobs_ref[near] = s + 64 * second + 4096 * first
        jobs_ref[near + 1] = s + SLOTS + 64 * first + 4096 * second
        jobs_ref[LISTS + far] = s + SLOTS + 64 * first + 4096 * out
        jobs_ref[2 * LISTS + far] = s + 64 * out + 4096 * rim
        return near + 2 * local, far + 1 - local

    near, far = lax.fori_loop(0, count, listed, (jnp.int32(0), jnp.int32(0)))
    for j in range(8):
        jobs_ref[near + j] = 4096 * ATOMS
        jobs_ref[LISTS + far + j] = 4096 * 4
        jobs_ref[2 * LISTS + far + j] = 4096 * 4
    jobs_ref[3 * LISTS] = near
    jobs_ref[3 * LISTS + 1] = far

    coup = coup_ref[...].astype(F32)
    width = 7 * LANES
    coup = jnp.concatenate([coup, jnp.zeros((SLOTS, width - MODES * SQ), F32)], axis=1)
    lane = iota((SLOTS, LANES), 1)
    for m in range(MODES):
        part = coup if m == 0 else pltpu.roll(coup, width - m * SQ, 1)
        cm[m * SLOTS : (m + 1) * SLOTS, :] = jnp.where(lane < SQ, part[:, :LANES], 0.0)

    ij = iota((LANES, LANES), 0)
    jk = iota((LANES, LANES), 1)
    valid = (ij < SQ) & (jk < SQ)
    row = iota((16, LANES), 0) % NORB
    col = iota((16, LANES), 1)
    sub = iota((8, LANES), 0)

    def expand(keep, other, at):
        spread = jnp.concatenate(
            [
                jnp.where(valid & (other == jk // NORB), 1.0, 0.0),
                jnp.where(valid & (other == jk % NORB), 1.0, 0.0),
            ],
            axis=1,
        ).astype(BF)
        keep = jnp.where(keep == row, 1.0, 0.0)

        def fill(s, carry):
            for m in range(MODES):
                line = cm[pl.ds(m * SLOTS + s, 1), :]
                v[pl.ds(pl.multiple_of(s * (16 * MODES) + m * 16, 16), 16), :] = (
                    jnp.broadcast_to(line, (16, LANES)) * keep
                ).astype(BF)
            return carry

        lax.fori_loop(0, count, fill, 0)
        for part in range(SLOTS // 2):
            lo = part * 32 * MODES
            c12[lo : lo + 32 * MODES, :] = jnp.dot(
                v[lo : lo + 32 * MODES, :], spread, preferred_element_type=F32
            )

        def product(s, carry):
            for m in range(MODES):
                base = pl.multiple_of(s * (16 * MODES) + m * 16, 16)
                first = c12[pl.ds(base, 16), :LANES]
                second = c12[pl.ds(base, 16), LANES:]
                turns = [
                    second[0:8],
                    second[8:16],
                    pltpu.roll(second, 10, 0)[0:8],
                    pltpu.roll(second, 12, 0)[0:8],
                    pltpu.roll(second, 14, 0)[0:8],
                ]
                spreads = [jnp.broadcast_to(first[i : i + 1], (8, LANES)) for i in range(NORB)]
                rows = []
                for g in range(ROWS // 8):
                    lo = 8 * g // NORB
                    hi = min((8 * g + 7) // NORB, NORB - 1)
                    left = spreads[lo]
                    if hi != lo:
                        left = jnp.where(sub < NORB * hi - 8 * g, left, spreads[hi])
                    rows.append(left * turns[g % 5])
                t_ref[at + s, :, m * LANES : (m + 1) * LANES] = jnp.concatenate(rows, axis=0).astype(BF)
            return carry

        lax.fori_loop(0, count, product, 0)

    expand(col // NORB, ij % NORB, 0)
    expand(col % NORB, ij // NORB, SLOTS)

    odd = lax.axis_index("energy") % 2
    e_in = iota((2 * LANES, LANES), 0)
    e_out = iota((2 * LANES, LANES), 1)
    left_first = jnp.where(e_in < 128, e_in, jnp.where(e_in < 192, e_in - 192, e_in - 64))
    right_first = jnp.where(e_in < 128, e_in, jnp.where(e_in < 192, e_in, e_in - 256))
    orders = (jnp.where(odd == 1, left_first, right_first), jnp.where(odd == 1, right_first, left_first))
    for m in range(MODES):
        occ = occ_ref[m]
        step = off_ref[m]
        for which in range(2):
            away = orders[which] - e_out
            s_ref[which, :, m * LANES : (m + 1) * LANES] = jnp.where(
                away == -step, occ, jnp.where(away == step, occ + 1.0, 0.0)
            ).astype(BF)


def shift_atom(center, halo, s_ref, which, lhs, low, store):
    lhs[0:ROWS, :LANES] = center[0:ROWS]
    lhs[0:ROWS, LANES:] = halo[0:ROWS]
    low[0:ROWS, :LANES] = center[96:SLAB].astype(F32)
    low[0:ROWS, LANES:] = halo[96:SLAB].astype(F32)
    low[ROWS:, :] = jnp.zeros((PITCH - ROWS, 256), F32)
    lhs[PITCH : PITCH + ROWS, :] = low[4 : 4 + ROWS, :].astype(BF)
    for t in range(MODES // 2):
        out = jnp.dot(lhs[...], s_ref[which, :, t * 256 : (t + 1) * 256], preferred_element_type=F32)
        for mm in range(2):
            for r in range(2):
                store(
                    2 * t + mm,
                    r,
                    out[r * PITCH : r * PITCH + ROWS, mm * LANES : (mm + 1) * LANES].astype(BF),
                )


def halo_of(from_a, from_b, x):
    left = iota((SLAB, LANES), 1) < KMAX
    a = from_a[x % 4]
    b = from_b[x % 4]
    return jnp.where(left, a, b) if x < 4 else jnp.where(left, b, a)


def store_in(x_ref, at):
    def store(m, r, value):
        x_ref[at, m * LANES : m * LANES + ROWS, r * LANES : (r + 1) * LANES] = value

    return store


def unfold(total, rows):
    rows[0:ROWS, :] = total[:, :LANES]
    rows[SQ : SQ + ROWS, :] = total[:, LANES:]
    return rows[0:SLAB, :]


def run_jobs(jobs_ref, at, count, chunk, t_ref, x_ref, acc):
    def step(i, carry):
        for j in range(chunk):
            job = jobs_ref[at + i * chunk + j]
            t, src, dst = job & 63, (job >> 6) & 63, job >> 12
            acc[dst] = acc[dst] + jnp.dot(t_ref[t], x_ref[src], preferred_element_type=F32)
        return carry

    lax.fori_loop(0, (count + chunk - 1) // chunk, step, 0)


def rim_kernel(
    jobs_ref, g_ref, from_b, from_a, s_ref, t_ref, x_old, cross_ref, near_ref, x, part, lhs, low, rows
):
    halos = []
    for at, atom in enumerate((0, 1, 6, 7)):
        halo = halo_of(from_a, from_b, atom)
        halos.append(halo)
        shift_atom(g_ref[atom], halo, s_ref, atom // 4, lhs.at[at], low.at[at], store_in(x, atom))
    part[...] = jnp.zeros(part.shape, F32)
    run_jobs(jobs_ref, LISTS, jobs_ref[3 * LISTS + 1], 4, t_ref, x, part)
    odd = lax.axis_index("atom") % 2

    def fill(ref, side):
        for j in range(2):
            ref[j] = g_ref[6 * side + j]
            ref[2 + j] = halos[2 * side + j]
            ref[4 + j] = unfold(part[2 * side + j], rows).astype(BF)

    @pl.when(odd == 1)
    def _():
        fill(cross_ref, 1)
        fill(near_ref, 0)

    @pl.when(odd == 0)
    def _():
        fill(cross_ref, 0)
        fill(near_ref, 1)


def local_kernel(
    jobs_ref, g_ref, from_b, from_a, s_ref, t_ref, x_old, inner_ref, rim_ref, x, acc, lhs, low, rows
):
    for at, atom in enumerate((2, 3, 4, 5)):
        halo = halo_of(from_a, from_b, atom)
        shift_atom(g_ref[atom], halo, s_ref, atom // 4, lhs.at[at], low.at[at], store_in(x, atom))
    acc[...] = jnp.zeros(acc.shape, F32)
    run_jobs(jobs_ref, 0, jobs_ref[3 * LISTS], 8, t_ref, x, acc)
    for j in range(4):
        inner_ref[j] = unfold(acc[2 + j], rows).astype(BF)
        rim_ref[j] = acc[j if j < 2 else j + 4]


def final_kernel(
    jobs_ref, cross_ref, near_ref, s_ref, t_ref, inner_ref, rim_ref, x_old, out_ref, x, acc, done, lhs, low, rows, sems
):
    early = pltpu.make_async_copy(inner_ref, out_ref.at[2:6], sems.at[0])
    early.start()
    odd = lax.axis_index("atom") % 2

    def take(ref, side):
        for j in range(2):
            at = 2 * side + j
            shift_atom(ref[j], ref[2 + j], s_ref, 1 - side, lhs.at[at], low.at[at], store_in(x, at))

    @pl.when(odd == 1)
    def _():
        take(cross_ref, 1)
        take(near_ref, 0)

    @pl.when(odd == 0)
    def _():
        take(cross_ref, 0)
        take(near_ref, 1)

    acc[0:4] = rim_ref[...]
    run_jobs(jobs_ref, 2 * LISTS, jobs_ref[3 * LISTS + 1], 4, t_ref, x, acc)
    for j in range(4):
        side = j // 2
        got = jnp.where(
            odd == side, cross_ref[4 + j % 2].astype(F32), near_ref[4 + j % 2].astype(F32)
        )
        done[j] = (unfold(acc[j], rows) + got).astype(BF)
    lower = pltpu.make_async_copy(done.at[0:2], out_ref.at[0:2], sems.at[1])
    upper = pltpu.make_async_copy(done.at[2:4], out_ref.at[6:8], sems.at[2])
    lower.start()
    upper.start()
    early.wait()
    lower.wait()
    upper.wait()


def swap(value, axis, start):
    count = lax.axis_size(axis)
    pairs = [(i, i + 1) for i in range(start, count - 1, 2)]
    return lax.ppermute(value, axis, pairs + [(b, a) for a, b in pairs])


def call(kernel, outs, scratch, flops, moved, specs, out_specs, aliases={}):
    return pl.pallas_call(
        kernel,
        out_shape=outs,
        in_specs=specs,
        out_specs=out_specs,
        scratch_shapes=scratch,
        input_output_aliases=aliases,
        compiler_params=pltpu.CompilerParams(vmem_limit_bytes=32 * 1024 * 1024),
        cost_estimate=pl.CostEstimate(flops=flops, bytes_accessed=moved, transcendentals=0),
    )


def per_device(green, coupling, pairs, counts, occupation, offsets):
    atoms, slab, e_dev = green.shape
    shape = jax.ShapeDtypeStruct
    dma = pltpu.SemaphoreType.DMA
    pairs = pairs.T

    half = shape((atoms // 2, slab, e_dev), BF)
    taken = (green, coupling, pairs, occupation, offsets)
    to_a, to_b, g, coup, pairs, occ, off = call(
        pack_kernel,
        (half, half) + tuple(shape(v.shape, v.dtype) for v in taken),
        [dma((5,))],
        int(1e6),
        int(1e6),
        [HBM] * 5,
        (VMEM,) * 7,
    )(*[pltpu.with_memory_space_constraint(v, pltpu.HBM) for v in taken])
    from_b = swap(to_b, "energy", 1)
    from_a = swap(to_a, "energy", 0)

    shifted = shape((ATOMS, DEPTH, 256), BF)
    t, s, jobs, x = call(
        build_kernel,
        (shape((2 * SLOTS, ROWS, DEPTH), BF), shape((2, 256, DEPTH), BF), shape((3 * LISTS + 8,), I32), shifted),
        [
            pltpu.VMEM((MODES * SLOTS, LANES), F32),
            pltpu.VMEM((MODES * SLOTS * 16, LANES), BF),
            pltpu.VMEM((MODES * SLOTS * 16, 256), F32),
        ],
        int(3e9),
        int(8e6),
        [SMEM] * 4 + [VMEM],
        (VMEM, VMEM, SMEM, VMEM),
    )(counts, pairs, occ, off, coup)

    spare = [
        pltpu.VMEM((4, 2 * PITCH, 256), BF),
        pltpu.VMEM((4, PITCH, 256), F32),
        pltpu.VMEM((208, LANES), F32),
    ]
    payload = shape((6, slab, e_dev), BF)
    cross, near, x = call(
        rim_kernel,
        (payload, payload, shifted),
        [pltpu.VMEM((5, ROWS, 256), F32)] + spare,
        int(1e9),
        int(1e6),
        [SMEM] + [VMEM] * 6,
        (VMEM, VMEM, VMEM),
        {6: 2},
    )(jobs, g, from_b, from_a, s, t, x)
    cross = swap(cross, "atom", 1)
    near = swap(near, "atom", 0)

    inner, rim, x = call(
        local_kernel,
        (shape((4, slab, e_dev), BF), shape((4, ROWS, 256), F32), shifted),
        [pltpu.VMEM((9, ROWS, 256), F32)] + spare,
        int(3e9),
        int(1e6),
        [SMEM] + [VMEM] * 6,
        (VMEM, VMEM, VMEM),
        {6: 2},
    )(jobs, g, from_b, from_a, s, t, x)

    return call(
        final_kernel,
        (shape((atoms, slab, e_dev), BF), shifted),
        [pltpu.VMEM((5, ROWS, 256), F32), pltpu.VMEM((4, slab, e_dev), BF)] + spare + [dma((3,))],
        int(1e9),
        int(1e6),
        [SMEM] + [VMEM] * 7,
        (HBM, VMEM),
        {7: 1},
    )(jobs, cross, near, s, t, inner, rim, x)[0]


def solution(mesh):
    placed = (P("atom", None, "energy"), P("atom", None), P("atom", None), P("atom"), P(), P())
    return jax.shard_map(
        per_device, mesh=mesh, in_specs=placed, out_specs=P("atom", None, "energy"), check_vma=False
    )
```

```python
import jax
import jax.numpy as jnp
from jax import lax
from jax.experimental import pallas as pl
from jax.experimental.pallas import tpu as pltpu
from jax.sharding import PartitionSpec as P

NORB = 10
MODES = 8
KMAX = 64
SQ = NORB * NORB
ROWS = 104
PITCH = 112
LANES = 128
DEPTH = MODES * LANES
SLOTS = 16
ATOMS = 8
SLAB = 2 * SQ
LISTS = 48
BF = jnp.bfloat16
F32 = jnp.float32
I32 = jnp.int32
VMEM = pl.BlockSpec(memory_space=pltpu.VMEM)
SMEM = pl.BlockSpec(memory_space=pltpu.SMEM)
HBM = pl.BlockSpec(memory_space=pltpu.HBM)


def iota(shape, dim):
    return lax.broadcasted_iota(I32, shape, dim)


def pack_kernel(g_hbm, coup_hbm, pairs_hbm, occ_hbm, off_hbm, to_a, to_b, g, coup, pairs, occ, off, sems):
    half = ATOMS // 2
    moves = ((g_hbm, g), (coup_hbm, coup), (pairs_hbm, pairs), (occ_hbm, occ), (off_hbm, off))
    copies = [pltpu.make_async_copy(src, dst, sems.at[i]) for i, (src, dst) in enumerate(moves)]
    for copy in copies:
        copy.start()
    odd = lax.axis_index("energy") % 2
    pick = (iota((SLAB, LANES), 1) // KMAX) == odd
    copies[0].wait()
    for x in range(half):
        turned = pltpu.roll(g[x + half * odd].astype(F32), KMAX, 1).astype(BF)
        kept = g[x + half - half * odd]
        to_a[x] = jnp.where(pick, turned, kept)
        to_b[x] = jnp.where(pick, kept, turned)
    for copy in copies[1:]:
        copy.wait()


def build_kernel(cnt_ref, pairs_ref, occ_ref, off_ref, coup_ref, t_ref, s_ref, jobs_ref, x_ref, cm, v, c12):
    count = cnt_ref[0]
    base = lax.axis_index("atom") * ATOMS
    for x in range(ATOMS):
        for m in range(MODES):
            x_ref[x, m * LANES + 96 : (m + 1) * LANES, :] = jnp.zeros((32, 256), BF)

    def listed(s, carry):
        near, far, down, up = carry
        first = pairs_ref[0, s] - base
        second = pairs_ref[1, s] - base
        local = jnp.where((second >= 0) & (second < ATOMS), 1, 0)
        below = jnp.where(second < 0, 1, 0)
        out = jnp.where(second < 0, second + 2, second - 6)
        jobs_ref[near] = s + 64 * second + 4096 * first
        jobs_ref[near + 1] = s + SLOTS + 64 * first + 4096 * second
        jobs_ref[LISTS + far] = s + SLOTS + 64 * first + 4096 * out
        jobs_ref[2 * LISTS + down] = s + 64 * out + 4096 * first
        jobs_ref[3 * LISTS + up] = s + 64 * out + 4096 * (first - 6)
        return near + 2 * local, far + 1 - local, down + below, up + 1 - local - below

    counted = lax.fori_loop(0, count, listed, (jnp.int32(0),) * 4)
    for kind, (many, spare) in enumerate(zip(counted, (ATOMS, 4, 2, 2))):
        for j in range(8):
            jobs_ref[kind * LISTS + many + j] = 4096 * spare
        jobs_ref[4 * LISTS + kind] = many

    coup = coup_ref[...].astype(F32)
    width = 7 * LANES
    coup = jnp.concatenate([coup, jnp.zeros((SLOTS, width - MODES * SQ), F32)], axis=1)
    lane = iota((SLOTS, LANES), 1)
    for m in range(MODES):
        part = coup if m == 0 else pltpu.roll(coup, width - m * SQ, 1)
        cm[m * SLOTS : (m + 1) * SLOTS, :] = jnp.where(lane < SQ, part[:, :LANES], 0.0)

    ij = iota((LANES, LANES), 0)
    jk = iota((LANES, LANES), 1)
    valid = (ij < SQ) & (jk < SQ)
    row = iota((16, LANES), 0) % NORB
    col = iota((16, LANES), 1)
    sub = iota((8, LANES), 0)

    def expand(keep, other, at):
        spread = jnp.concatenate(
            [
                jnp.where(valid & (other == jk // NORB), 1.0, 0.0),
                jnp.where(valid & (other == jk % NORB), 1.0, 0.0),
            ],
            axis=1,
        ).astype(BF)
        keep = jnp.where(keep == row, 1.0, 0.0)

        def fill(s, carry):
            for m in range(MODES):
                line = cm[pl.ds(m * SLOTS + s, 1), :]
                v[pl.ds(pl.multiple_of(s * (16 * MODES) + m * 16, 16), 16), :] = (
                    jnp.broadcast_to(line, (16, LANES)) * keep
                ).astype(BF)
            return carry

        lax.fori_loop(0, count, fill, 0)
        for part in range(SLOTS // 2):
            lo = part * 32 * MODES
            c12[lo : lo + 32 * MODES, :] = jnp.dot(
                v[lo : lo + 32 * MODES, :], spread, preferred_element_type=F32
            )

        def product(s, carry):
            for m in range(MODES):
                base = pl.multiple_of(s * (16 * MODES) + m * 16, 16)
                first = c12[pl.ds(base, 16), :LANES]
                second = c12[pl.ds(base, 16), LANES:]
                turns = [
                    second[0:8],
                    second[8:16],
                    pltpu.roll(second, 10, 0)[0:8],
                    pltpu.roll(second, 12, 0)[0:8],
                    pltpu.roll(second, 14, 0)[0:8],
                ]
                spreads = [jnp.broadcast_to(first[i : i + 1], (8, LANES)) for i in range(NORB)]
                rows = []
                for g in range(ROWS // 8):
                    lo = 8 * g // NORB
                    hi = min((8 * g + 7) // NORB, NORB - 1)
                    left = spreads[lo]
                    if hi != lo:
                        left = jnp.where(sub < NORB * hi - 8 * g, left, spreads[hi])
                    rows.append(left * turns[g % 5])
                t_ref[at + s, :, m * LANES : (m + 1) * LANES] = jnp.concatenate(rows, axis=0).astype(BF)
            return carry

        lax.fori_loop(0, count, product, 0)

    expand(col // NORB, ij % NORB, 0)
    expand(col % NORB, ij // NORB, SLOTS)

    odd = lax.axis_index("energy") % 2
    e_in = iota((2 * LANES, LANES), 0)
    e_out = iota((2 * LANES, LANES), 1)
    left_first = jnp.where(e_in < 128, e_in, jnp.where(e_in < 192, e_in - 192, e_in - 64))
    right_first = jnp.where(e_in < 128, e_in, jnp.where(e_in < 192, e_in, e_in - 256))
    orders = (jnp.where(odd == 1, left_first, right_first), jnp.where(odd == 1, right_first, left_first))
    for m in range(MODES):
        occ = occ_ref[m]
        step = off_ref[m]
        for which in range(2):
            away = orders[which] - e_out
            s_ref[which, :, m * LANES : (m + 1) * LANES] = jnp.where(
                away == -step, occ, jnp.where(away == step, occ + 1.0, 0.0)
            ).astype(BF)


def shift_atom(center, halo, s_ref, which, lhs, low, store):
    lhs[0:ROWS, :LANES] = center[0:ROWS]
    lhs[0:ROWS, LANES:] = halo[0:ROWS]
    low[0:ROWS, :LANES] = center[96:SLAB].astype(F32)
    low[0:ROWS, LANES:] = halo[96:SLAB].astype(F32)
    low[ROWS:, :] = jnp.zeros((PITCH - ROWS, 256), F32)
    lhs[PITCH : PITCH + ROWS, :] = low[4 : 4 + ROWS, :].astype(BF)
    for t in range(MODES // 2):
        out = jnp.dot(lhs[...], s_ref[which, :, t * 256 : (t + 1) * 256], preferred_element_type=F32)
        for mm in range(2):
            for r in range(2):
                store(
                    2 * t + mm,
                    r,
                    out[r * PITCH : r * PITCH + ROWS, mm * LANES : (mm + 1) * LANES].astype(BF),
                )


def halo_of(from_a, from_b, x):
    left = iota((SLAB, LANES), 1) < KMAX
    a = from_a[x % 4]
    b = from_b[x % 4]
    return jnp.where(left, a, b) if x < 4 else jnp.where(left, b, a)


def store_in(x_ref, at):
    def store(m, r, value):
        x_ref[at, m * LANES : m * LANES + ROWS, r * LANES : (r + 1) * LANES] = value

    return store


def unfold(total, rows):
    rows[0:ROWS, :] = total[:, :LANES]
    rows[SQ : SQ + ROWS, :] = total[:, LANES:]
    return rows[0:SLAB, :]


def run_jobs(jobs_ref, kind, chunk, t_ref, x_ref, acc):
    count = jobs_ref[4 * LISTS + kind]

    def step(i, carry):
        for j in range(chunk):
            job = jobs_ref[kind * LISTS + i * chunk + j]
            t, src, dst = job & 63, (job >> 6) & 63, job >> 12
            acc[dst] = acc[dst] + jnp.dot(t_ref[t], x_ref[src], preferred_element_type=F32)
        return carry

    lax.fori_loop(0, (count + chunk - 1) // chunk, step, 0)


def rim_kernel(
    jobs_ref, g_ref, from_b, from_a, s_ref, t_ref, x_old, down_ref, up_ref, x, part, lhs, low, rows
):
    for at, atom in enumerate((0, 1, 6, 7)):
        ref = up_ref if atom >= 6 else down_ref
        halo = halo_of(from_a, from_b, atom)
        ref[at % 2] = g_ref[atom]
        ref[2 + at % 2] = halo
        shift_atom(g_ref[atom], halo, s_ref, atom // 4, lhs.at[at], low.at[at], store_in(x, atom))
    part[...] = jnp.zeros(part.shape, F32)
    run_jobs(jobs_ref, 1, 4, t_ref, x, part)
    for at in range(4):
        ref = up_ref if at >= 2 else down_ref
        ref[4 + at % 2] = unfold(part[at], rows.at[at]).astype(BF)


def local_kernel(
    jobs_ref, g_ref, from_b, from_a, s_ref, t_ref, x_old, inner_ref, rim_ref, x, acc, lhs, low, rows
):
    for at, atom in enumerate((2, 3, 4, 5)):
        halo = halo_of(from_a, from_b, atom)
        shift_atom(g_ref[atom], halo, s_ref, atom // 4, lhs.at[at], low.at[at], store_in(x, atom))
    acc[...] = jnp.zeros(acc.shape, F32)
    run_jobs(jobs_ref, 0, 8, t_ref, x, acc)
    for j in range(4):
        inner_ref[j] = unfold(acc[2 + j], rows.at[j]).astype(BF)
        rim_ref[j] = acc[j if j < 2 else j + 4]


def upper_kernel(jobs_ref, got_ref, s_ref, t_ref, rim_ref, x_old, out_ref, x, acc, lhs, low, rows):
    for j in range(2):
        shift_atom(got_ref[j], got_ref[2 + j], s_ref, 0, lhs.at[j], low.at[j], store_in(x, 2 + j))
    acc[0:2] = rim_ref[2:4]
    run_jobs(jobs_ref, 3, 4, t_ref, x, acc)
    for j in range(2):
        out_ref[j] = (unfold(acc[j], rows.at[j]) + got_ref[4 + j].astype(F32)).astype(BF)


def lower_kernel(
    jobs_ref, got_ref, s_ref, t_ref, rim_ref, inner_ref, upper_ref, x_old, out_ref, x, acc, done, lhs, low, rows, sems
):
    copies = [
        pltpu.make_async_copy(inner_ref, out_ref.at[2:6], sems.at[0]),
        pltpu.make_async_copy(upper_ref, out_ref.at[6:8], sems.at[1]),
        pltpu.make_async_copy(done, out_ref.at[0:2], sems.at[2]),
    ]
    copies[0].start()
    copies[1].start()
    for j in range(2):
        shift_atom(got_ref[j], got_ref[2 + j], s_ref, 1, lhs.at[j], low.at[j], store_in(x, j))
    acc[0:2] = rim_ref[0:2]
    run_jobs(jobs_ref, 2, 4, t_ref, x, acc)
    for j in range(2):
        done[j] = (unfold(acc[j], rows.at[j]) + got_ref[4 + j].astype(F32)).astype(BF)
    copies[2].start()
    for copy in copies:
        copy.wait()


def swap(value, axis, start):
    count = lax.axis_size(axis)
    pairs = [(i, i + 1) for i in range(start, count - 1, 2)]
    return lax.ppermute(value, axis, pairs + [(b, a) for a, b in pairs])


def step_of(value, axis, by):
    count = lax.axis_size(axis)
    return lax.ppermute(value, axis, [(i, i + by) for i in range(count) if 0 <= i + by < count])


def call(kernel, outs, scratch, flops, moved, specs, out_specs, aliases={}):
    return pl.pallas_call(
        kernel,
        out_shape=outs,
        in_specs=specs,
        out_specs=out_specs,
        scratch_shapes=scratch,
        input_output_aliases=aliases,
        compiler_params=pltpu.CompilerParams(vmem_limit_bytes=32 * 1024 * 1024),
        cost_estimate=pl.CostEstimate(flops=flops, bytes_accessed=moved, transcendentals=0),
    )


def per_device(green, coupling, pairs, counts, occupation, offsets):
    atoms, slab, e_dev = green.shape
    shape = jax.ShapeDtypeStruct
    dma = pltpu.SemaphoreType.DMA
    pairs = pairs.T

    half = shape((atoms // 2, slab, e_dev), BF)
    taken = (green, coupling, pairs, occupation, offsets)
    to_a, to_b, g, coup, pairs, occ, off = call(
        pack_kernel,
        (half, half) + tuple(shape(v.shape, v.dtype) for v in taken),
        [dma((5,))],
        int(1e6),
        int(1e6),
        [HBM] * 5,
        (VMEM,) * 7,
    )(*[pltpu.with_memory_space_constraint(v, pltpu.HBM) for v in taken])
    from_b = swap(to_b, "energy", 1)
    from_a = swap(to_a, "energy", 0)

    shifted = shape((ATOMS, DEPTH, 256), BF)
    t, s, jobs, x = call(
        build_kernel,
        (shape((2 * SLOTS, ROWS, DEPTH), BF), shape((2, 256, DEPTH), BF), shape((4 * LISTS + 4,), I32), shifted),
        [
            pltpu.VMEM((MODES * SLOTS, LANES), F32),
            pltpu.VMEM((MODES * SLOTS * 16, LANES), BF),
            pltpu.VMEM((MODES * SLOTS * 16, 256), F32),
        ],
        int(3e9),
        int(8e6),
        [SMEM] * 4 + [VMEM],
        (VMEM, VMEM, SMEM, VMEM),
    )(counts, pairs, occ, off, coup)

    spare = [
        pltpu.VMEM((4, 2 * PITCH, 256), BF),
        pltpu.VMEM((4, PITCH, 256), F32),
        pltpu.VMEM((4, 208, LANES), F32),
    ]
    payload = shape((6, slab, e_dev), BF)
    down, up, x = call(
        rim_kernel,
        (payload, payload, shifted),
        [pltpu.VMEM((5, ROWS, 256), F32)] + spare,
        int(1e9),
        int(1e6),
        [SMEM] + [VMEM] * 6,
        (VMEM, VMEM, VMEM),
        {6: 2},
    )(jobs, g, from_b, from_a, s, t, x)
    above = step_of(down, "atom", -1)
    below = step_of(up, "atom", 1)

    inner, rim, x = call(
        local_kernel,
        (shape((4, slab, e_dev), BF), shape((4, ROWS, 256), F32), shifted),
        [pltpu.VMEM((9, ROWS, 256), F32)] + spare,
        int(3e9),
        int(1e6),
        [SMEM] + [VMEM] * 6,
        (VMEM, VMEM, VMEM),
        {6: 2},
    )(jobs, g, from_b, from_a, s, t, x)

    sums = pltpu.VMEM((3, ROWS, 256), F32)
    upper, x = call(
        upper_kernel,
        (shape((2, slab, e_dev), BF), shifted),
        [sums] + spare,
        int(5e8),
        int(1e6),
        [SMEM] + [VMEM] * 5,
        (VMEM, VMEM),
        {5: 1},
    )(jobs, above, s, t, rim, x)

    return call(
        lower_kernel,
        (shape((atoms, slab, e_dev), BF), shifted),
        [sums, pltpu.VMEM((2, slab, e_dev), BF)] + spare + [dma((3,))],
        int(5e8),
        int(1e6),
        [SMEM] + [VMEM] * 7,
        (HBM, VMEM),
        {7: 1},
    )(jobs, below, s, t, rim, inner, upper, x)[0]


def solution(mesh):
    placed = (P("atom", None, "energy"), P("atom", None), P("atom", None), P("atom"), P(), P())
    return jax.shard_map(
        per_device, mesh=mesh, in_specs=placed, out_specs=P("atom", None, "energy"), check_vma=False
    )
```

```python
import jax
import jax.numpy as jnp
from jax import lax
from jax.experimental import pallas as pl
from jax.experimental.pallas import tpu as pltpu
from jax.sharding import PartitionSpec as P

NORB = 10
MODES = 8
KMAX = 64
SQ = NORB * NORB
ROWS = 104
PITCH = 112
LANES = 128
DEPTH = MODES * LANES
SLOTS = 16
ATOMS = 8
SLAB = 2 * SQ
LISTS = 48
BF = jnp.bfloat16
F32 = jnp.float32
I32 = jnp.int32
VMEM = pl.BlockSpec(memory_space=pltpu.VMEM)
SMEM = pl.BlockSpec(memory_space=pltpu.SMEM)
HBM = pl.BlockSpec(memory_space=pltpu.HBM)


def iota(shape, dim):
    return lax.broadcasted_iota(I32, shape, dim)


def pack_kernel(g_hbm, coup_hbm, pairs_hbm, occ_hbm, off_hbm, to_a, to_b, g, coup, pairs, occ, off, sems):
    half = ATOMS // 2
    moves = ((g_hbm, g), (coup_hbm, coup), (pairs_hbm, pairs), (occ_hbm, occ), (off_hbm, off))
    copies = [pltpu.make_async_copy(src, dst, sems.at[i]) for i, (src, dst) in enumerate(moves)]
    for copy in copies:
        copy.start()
    odd = lax.axis_index("energy") % 2
    pick = (iota((SLAB, LANES), 1) // KMAX) == odd
    copies[0].wait()
    for x in range(half):
        turned = pltpu.roll(g[x + half * odd].astype(F32), KMAX, 1).astype(BF)
        kept = g[x + half - half * odd]
        to_a[x] = jnp.where(pick, turned, kept)
        to_b[x] = jnp.where(pick, kept, turned)
    for copy in copies[1:]:
        copy.wait()


def build_kernel(
    cnt_ref, pairs_in, occ_in, off_in, coup_ref, t_ref, s_ref, jobs_out, x_ref, cm, v, c12, pairs_ref, occ_ref, off_ref, jobs_ref, sems
):
    moves = ((pairs_in, pairs_ref), (occ_in, occ_ref), (off_in, off_ref))
    copies = [pltpu.make_async_copy(src, dst, sems.at[i]) for i, (src, dst) in enumerate(moves)]
    for copy in copies:
        copy.start()
    count = cnt_ref[0]
    base = lax.axis_index("atom") * ATOMS
    for x in range(ATOMS):
        for m in range(MODES):
            x_ref[x, m * LANES + 96 : (m + 1) * LANES, :] = jnp.zeros((32, 256), BF)

    def listed(s, carry):
        near, far, down, up = carry
        first = pairs_ref[0, s] - base
        second = pairs_ref[1, s] - base
        local = jnp.where((second >= 0) & (second < ATOMS), 1, 0)
        below = jnp.where(second < 0, 1, 0)
        out = jnp.where(second < 0, second + 2, second - 6)
        jobs_ref[near] = s + 64 * second + 4096 * first
        jobs_ref[near + 1] = s + SLOTS + 64 * first + 4096 * second
        jobs_ref[LISTS + far] = s + SLOTS + 64 * first + 4096 * out
        jobs_ref[2 * LISTS + down] = s + 64 * out + 4096 * first
        jobs_ref[3 * LISTS + up] = s + 64 * out + 4096 * (first - 6)
        return near + 2 * local, far + 1 - local, down + below, up + 1 - local - below

    for copy in copies:
        copy.wait()
    counted = lax.fori_loop(0, count, listed, (jnp.int32(0),) * 4)
    for kind, (many, spare) in enumerate(zip(counted, (ATOMS, 4, 2, 2))):
        for j in range(8):
            jobs_ref[kind * LISTS + many + j] = 4096 * spare
        jobs_ref[4 * LISTS + kind] = many
    send = pltpu.make_async_copy(jobs_ref, jobs_out, sems.at[3])
    send.start()

    coup = coup_ref[...].astype(F32)
    width = 7 * LANES
    coup = jnp.concatenate([coup, jnp.zeros((SLOTS, width - MODES * SQ), F32)], axis=1)
    lane = iota((SLOTS, LANES), 1)
    for m in range(MODES):
        part = coup if m == 0 else pltpu.roll(coup, width - m * SQ, 1)
        cm[m * SLOTS : (m + 1) * SLOTS, :] = jnp.where(lane < SQ, part[:, :LANES], 0.0)

    ij = iota((LANES, LANES), 0)
    jk = iota((LANES, LANES), 1)
    valid = (ij < SQ) & (jk < SQ)
    row = iota((16, LANES), 0) % NORB
    col = iota((16, LANES), 1)
    sub = iota((8, LANES), 0)

    def expand(keep, other, at):
        spread = jnp.concatenate(
            [
                jnp.where(valid & (other == jk // NORB), 1.0, 0.0),
                jnp.where(valid & (other == jk % NORB), 1.0, 0.0),
            ],
            axis=1,
        ).astype(BF)
        keep = jnp.where(keep == row, 1.0, 0.0)

        def fill(s, carry):
            for m in range(MODES):
                line = cm[pl.ds(m * SLOTS + s, 1), :]
                v[pl.ds(pl.multiple_of(s * (16 * MODES) + m * 16, 16), 16), :] = (
                    jnp.broadcast_to(line, (16, LANES)) * keep
                ).astype(BF)
            return carry

        lax.fori_loop(0, count, fill, 0)
        for part in range(SLOTS // 2):
            lo = part * 32 * MODES
            c12[lo : lo + 32 * MODES, :] = jnp.dot(
                v[lo : lo + 32 * MODES, :], spread, preferred_element_type=F32
            )

        def product(s, carry):
            for m in range(MODES):
                base = pl.multiple_of(s * (16 * MODES) + m * 16, 16)
                first = c12[pl.ds(base, 16), :LANES]
                second = c12[pl.ds(base, 16), LANES:]
                turns = [
                    second[0:8],
                    second[8:16],
                    pltpu.roll(second, 10, 0)[0:8],
                    pltpu.roll(second, 12, 0)[0:8],
                    pltpu.roll(second, 14, 0)[0:8],
                ]
                spreads = [jnp.broadcast_to(first[i : i + 1], (8, LANES)) for i in range(NORB)]
                rows = []
                for g in range(ROWS // 8):
                    lo = 8 * g // NORB
                    hi = min((8 * g + 7) // NORB, NORB - 1)
                    left = spreads[lo]
                    if hi != lo:
                        left = jnp.where(sub < NORB * hi - 8 * g, left, spreads[hi])
                    rows.append(left * turns[g % 5])
                t_ref[at + s, :, m * LANES : (m + 1) * LANES] = jnp.concatenate(rows, axis=0).astype(BF)
            return carry

        lax.fori_loop(0, count, product, 0)

    expand(col // NORB, ij % NORB, 0)
    expand(col % NORB, ij // NORB, SLOTS)

    odd = lax.axis_index("energy") % 2
    e_in = iota((2 * LANES, LANES), 0)
    e_out = iota((2 * LANES, LANES), 1)
    left_first = jnp.where(e_in < 128, e_in, jnp.where(e_in < 192, e_in - 192, e_in - 64))
    right_first = jnp.where(e_in < 128, e_in, jnp.where(e_in < 192, e_in, e_in - 256))
    orders = (jnp.where(odd == 1, left_first, right_first), jnp.where(odd == 1, right_first, left_first))
    for m in range(MODES):
        occ = occ_ref[m]
        step = off_ref[m]
        for which in range(2):
            away = orders[which] - e_out
            s_ref[which, :, m * LANES : (m + 1) * LANES] = jnp.where(
                away == -step, occ, jnp.where(away == step, occ + 1.0, 0.0)
            ).astype(BF)
    send.wait()


def shift_atom(center, halo, s_ref, which, lhs, low, store):
    lhs[0:ROWS, :LANES] = center[0:ROWS]
    lhs[0:ROWS, LANES:] = halo[0:ROWS]
    low[0:ROWS, :LANES] = center[96:SLAB].astype(F32)
    low[0:ROWS, LANES:] = halo[96:SLAB].astype(F32)
    low[ROWS:, :] = jnp.zeros((PITCH - ROWS, 256), F32)
    lhs[PITCH : PITCH + ROWS, :] = low[4 : 4 + ROWS, :].astype(BF)
    for t in range(MODES // 2):
        out = jnp.dot(lhs[...], s_ref[which, :, t * 256 : (t + 1) * 256], preferred_element_type=F32)
        for mm in range(2):
            for r in range(2):
                store(
                    2 * t + mm,
                    r,
                    out[r * PITCH : r * PITCH + ROWS, mm * LANES : (mm + 1) * LANES].astype(BF),
                )


def halo_of(from_a, from_b, x):
    left = iota((SLAB, LANES), 1) < KMAX
    a = from_a[x % 4]
    b = from_b[x % 4]
    return jnp.where(left, a, b) if x < 4 else jnp.where(left, b, a)


def store_in(x_ref, at):
    def store(m, r, value):
        x_ref[at, m * LANES : m * LANES + ROWS, r * LANES : (r + 1) * LANES] = value

    return store


def unfold(total, rows):
    rows[0:ROWS, :] = total[:, :LANES]
    rows[SQ : SQ + ROWS, :] = total[:, LANES:]
    return rows[0:SLAB, :]


class Lists:
    def __init__(self, source, held, sem):
        self.held = held
        self.copy = pltpu.make_async_copy(source, held, sem)
        self.copy.start()

    def ready(self):
        self.copy.wait()
        return self.held


def run_jobs(jobs_ref, kind, chunk, t_ref, x_ref, acc):
    count = jobs_ref[4 * LISTS + kind]

    def step(i, carry):
        for j in range(chunk):
            job = jobs_ref[kind * LISTS + i * chunk + j]
            t, src, dst = job & 63, (job >> 6) & 63, job >> 12
            acc[dst] = acc[dst] + jnp.dot(t_ref[t], x_ref[src], preferred_element_type=F32)
        return carry

    lax.fori_loop(0, (count + chunk - 1) // chunk, step, 0)


def rim_kernel(
    jobs_ref, g_ref, from_b, from_a, s_ref, t_ref, x_old, down_ref, up_ref, x, part, lhs, low, rows, held, sem
):
    lists = Lists(jobs_ref, held, sem)
    for at, atom in enumerate((0, 1, 6, 7)):
        ref = up_ref if atom >= 6 else down_ref
        halo = halo_of(from_a, from_b, atom)
        ref[at % 2] = g_ref[atom]
        ref[2 + at % 2] = halo
        shift_atom(g_ref[atom], halo, s_ref, atom // 4, lhs.at[at], low.at[at], store_in(x, atom))
    part[...] = jnp.zeros(part.shape, F32)
    run_jobs(lists.ready(), 1, 4, t_ref, x, part)
    for at in range(4):
        ref = up_ref if at >= 2 else down_ref
        ref[4 + at % 2] = unfold(part[at], rows.at[at]).astype(BF)


def early_kernel(
    jobs_ref, g_ref, from_b, from_a, s_ref, t_ref, x_old, up_old, inner_ref, rim_ref, x, up_ref, acc, lhs, low, rows, held, sem
):
    @pl.when(lax.axis_index("atom") % 2 == 1)
    def _():
        lists = Lists(jobs_ref, held, sem)
        local_terms(lists, g_ref, from_b, from_a, s_ref, t_ref, inner_ref, rim_ref, x, acc, lhs, low, rows)


def late_kernel(
    jobs_ref, g_ref, from_b, from_a, s_ref, t_ref, x_old, inner_old, rim_old, inner_ref, rim_ref, x, acc, lhs, low, rows, held, sem
):
    @pl.when(lax.axis_index("atom") % 2 == 0)
    def _():
        lists = Lists(jobs_ref, held, sem)
        local_terms(lists, g_ref, from_b, from_a, s_ref, t_ref, inner_ref, rim_ref, x, acc, lhs, low, rows)


def local_terms(lists, g_ref, from_b, from_a, s_ref, t_ref, inner_ref, rim_ref, x, acc, lhs, low, rows):
    for at, atom in enumerate((2, 3, 4, 5)):
        halo = halo_of(from_a, from_b, atom)
        shift_atom(g_ref[atom], halo, s_ref, atom // 4, lhs.at[at], low.at[at], store_in(x, atom))
    acc[...] = jnp.zeros(acc.shape, F32)
    run_jobs(lists.ready(), 0, 8, t_ref, x, acc)
    for j in range(4):
        inner_ref[j] = unfold(acc[2 + j], rows.at[j]).astype(BF)
        rim_ref[j] = acc[j if j < 2 else j + 4]


def upper_kernel(jobs_ref, got_ref, s_ref, t_ref, rim_ref, x_old, out_ref, x, acc, lhs, low, rows, held, sem):
    lists = Lists(jobs_ref, held, sem)
    for j in range(2):
        shift_atom(got_ref[j], got_ref[2 + j], s_ref, 0, lhs.at[j], low.at[j], store_in(x, 2 + j))
    acc[0:2] = rim_ref[2:4]
    run_jobs(lists.ready(), 3, 4, t_ref, x, acc)
    for j in range(2):
        out_ref[j] = (unfold(acc[j], rows.at[j]) + got_ref[4 + j].astype(F32)).astype(BF)


def lower_kernel(
    jobs_ref, got_ref, s_ref, t_ref, rim_ref, inner_ref, upper_ref, x_old, out_ref, x, acc, done, lhs, low, rows, held, sem, sems
):
    lists = Lists(jobs_ref, held, sem)
    copies = [
        pltpu.make_async_copy(inner_ref, out_ref.at[2:6], sems.at[0]),
        pltpu.make_async_copy(upper_ref, out_ref.at[6:8], sems.at[1]),
        pltpu.make_async_copy(done, out_ref.at[0:2], sems.at[2]),
    ]
    copies[0].start()
    copies[1].start()
    for j in range(2):
        shift_atom(got_ref[j], got_ref[2 + j], s_ref, 1, lhs.at[j], low.at[j], store_in(x, j))
    acc[0:2] = rim_ref[0:2]
    run_jobs(lists.ready(), 2, 4, t_ref, x, acc)
    for j in range(2):
        done[j] = (unfold(acc[j], rows.at[j]) + got_ref[4 + j].astype(F32)).astype(BF)
    copies[2].start()
    for copy in copies:
        copy.wait()


def swap(value, axis, start):
    count = lax.axis_size(axis)
    pairs = [(i, i + 1) for i in range(start, count - 1, 2)]
    return lax.ppermute(value, axis, pairs + [(b, a) for a, b in pairs])


def step_of(value, axis, by):
    count = lax.axis_size(axis)
    return lax.ppermute(value, axis, [(i, i + by) for i in range(count) if 0 <= i + by < count])


def call(kernel, outs, scratch, flops, moved, specs, out_specs, aliases={}):
    return pl.pallas_call(
        kernel,
        out_shape=outs,
        in_specs=specs,
        out_specs=out_specs,
        scratch_shapes=scratch,
        input_output_aliases=aliases,
        compiler_params=pltpu.CompilerParams(vmem_limit_bytes=32 * 1024 * 1024),
        cost_estimate=pl.CostEstimate(flops=flops, bytes_accessed=moved, transcendentals=0),
    )


def per_device(green, coupling, pairs, counts, occupation, offsets):
    atoms, slab, e_dev = green.shape
    shape = jax.ShapeDtypeStruct
    dma = pltpu.SemaphoreType.DMA
    pairs = pairs.T

    half = shape((atoms // 2, slab, e_dev), BF)
    taken = (green, coupling, pairs, occupation, offsets)
    to_a, to_b, g, coup, pairs, occ, off = call(
        pack_kernel,
        (half, half) + tuple(shape(v.shape, v.dtype) for v in taken),
        [dma((5,))],
        int(1e6),
        int(1e6),
        [HBM] * 5,
        (VMEM,) * 7,
    )(*[pltpu.with_memory_space_constraint(v, pltpu.HBM) for v in taken])
    from_b = swap(to_b, "energy", 1)
    from_a = swap(to_a, "energy", 0)

    shifted = shape((ATOMS, DEPTH, 256), BF)
    t, s, jobs, x = call(
        build_kernel,
        (shape((2 * SLOTS, ROWS, DEPTH), BF), shape((2, 256, DEPTH), BF), shape((4 * LISTS + 4,), I32), shifted),
        [
            pltpu.VMEM((MODES * SLOTS, LANES), F32),
            pltpu.VMEM((MODES * SLOTS * 16, LANES), BF),
            pltpu.VMEM((MODES * SLOTS * 16, 256), F32),
            pltpu.SMEM((2, SLOTS), I32),
            pltpu.SMEM((MODES,), F32),
            pltpu.SMEM((MODES,), I32),
            pltpu.SMEM((4 * LISTS + 4,), I32),
            dma((4,)),
        ],
        int(3e9),
        int(8e6),
        [SMEM] + [VMEM] * 4,
        (VMEM,) * 4,
    )(counts, pairs, occ, off, coup)

    spare = [
        pltpu.VMEM((4, 2 * PITCH, 256), BF),
        pltpu.VMEM((4, PITCH, 256), F32),
        pltpu.VMEM((4, 208, LANES), F32),
        pltpu.SMEM((4 * LISTS + 4,), I32),
        dma(()),
    ]
    payload = shape((6, slab, e_dev), BF)
    down, up, x = call(
        rim_kernel,
        (payload, payload, shifted),
        [pltpu.VMEM((5, ROWS, 256), F32)] + spare,
        int(1e9),
        int(1e6),
        [VMEM] * 7,
        (VMEM, VMEM, VMEM),
        {6: 2},
    )(jobs, g, from_b, from_a, s, t, x)
    above = step_of(down, "atom", -1)
    inner = shape((4, slab, e_dev), BF)
    rim = shape((4, ROWS, 256), F32)
    sums = pltpu.VMEM((9, ROWS, 256), F32)
    inner, rim, x, up = call(
        early_kernel,
        (inner, rim, shifted, payload),
        [sums] + spare,
        int(3e9),
        int(1e6),
        [VMEM] * 8,
        (VMEM,) * 4,
        {6: 2, 7: 3},
    )(jobs, g, from_b, from_a, s, t, x, up)
    below = step_of(up, "atom", 1)
    inner, rim, x = call(
        late_kernel,
        (shape(inner.shape, BF), shape(rim.shape, F32), shifted),
        [sums] + spare,
        int(3e9),
        int(1e6),
        [VMEM] * 9,
        (VMEM,) * 3,
        {7: 0, 8: 1, 6: 2},
    )(jobs, g, from_b, from_a, s, t, x, inner, rim)

    sums = pltpu.VMEM((3, ROWS, 256), F32)
    upper, x = call(
        upper_kernel,
        (shape((2, slab, e_dev), BF), shifted),
        [sums] + spare,
        int(5e8),
        int(1e6),
        [VMEM] * 6,
        (VMEM, VMEM),
        {5: 1},
    )(jobs, above, s, t, rim, x)

    return call(
        lower_kernel,
        (shape((atoms, slab, e_dev), BF), shifted),
        [sums, pltpu.VMEM((2, slab, e_dev), BF)] + spare + [dma((3,))],
        int(5e8),
        int(1e6),
        [VMEM] * 8,
        (HBM, VMEM),
        {7: 1},
    )(jobs, below, s, t, rim, inner, upper, x)[0]


def solution(mesh):
    placed = (P("atom", None, "energy"), P("atom", None), P("atom", None), P("atom"), P(), P())
    return jax.shard_map(
        per_device, mesh=mesh, in_specs=placed, out_specs=P("atom", None, "energy"), check_vma=False
    )
```

```python
import jax
import jax.numpy as jnp
from jax import lax
from jax.experimental import pallas as pl
from jax.experimental.pallas import tpu as pltpu
from jax.sharding import PartitionSpec as P

NORB = 10
MODES = 8
KMAX = 64
SQ = NORB * NORB
ROWS = 104
PITCH = 112
LANES = 128
DEPTH = MODES * LANES
SLOTS = 16
ATOMS = 8
SLAB = 2 * SQ
LISTS = 48
BF = jnp.bfloat16
F32 = jnp.float32
I32 = jnp.int32
VMEM = pl.BlockSpec(memory_space=pltpu.VMEM)
SMEM = pl.BlockSpec(memory_space=pltpu.SMEM)
HBM = pl.BlockSpec(memory_space=pltpu.HBM)


def iota(shape, dim):
    return lax.broadcasted_iota(I32, shape, dim)


def pack_kernel(g_hbm, coup_hbm, pairs_hbm, occ_hbm, off_hbm, to_a, to_b, g, coup, pairs, occ, off, sems):
    half = ATOMS // 2
    moves = ((g_hbm, g), (coup_hbm, coup), (pairs_hbm, pairs), (occ_hbm, occ), (off_hbm, off))
    copies = [pltpu.make_async_copy(src, dst, sems.at[i]) for i, (src, dst) in enumerate(moves)]
    for copy in copies:
        copy.start()
    odd = lax.axis_index("energy") % 2
    pick = (iota((SLAB, LANES), 1) // KMAX) == odd
    copies[0].wait()
    for x in range(half):
        turned = pltpu.roll(g[x + half * odd].astype(F32), KMAX, 1).astype(BF)
        kept = g[x + half - half * odd]
        to_a[x] = jnp.where(pick, turned, kept)
        to_b[x] = jnp.where(pick, kept, turned)
    for copy in copies[1:]:
        copy.wait()


def build_kernel(
    cnt_ref, pairs_in, occ_in, off_in, coup_ref, t_ref, s_ref, jobs_out, x_ref, cm, v, c12, pairs_ref, occ_ref, off_ref, jobs_ref, sems
):
    moves = ((pairs_in, pairs_ref), (occ_in, occ_ref), (off_in, off_ref))
    copies = [pltpu.make_async_copy(src, dst, sems.at[i]) for i, (src, dst) in enumerate(moves)]
    for copy in copies:
        copy.start()
    count = cnt_ref[0]
    base = lax.axis_index("atom") * ATOMS
    for x in range(ATOMS):
        for m in range(MODES):
            x_ref[x, m * LANES + 96 : (m + 1) * LANES, :] = jnp.zeros((32, 256), BF)

    def listed(s, carry):
        near, far, down, up = carry
        first = pairs_ref[0, s] - base
        second = pairs_ref[1, s] - base
        local = jnp.where((second >= 0) & (second < ATOMS), 1, 0)
        below = jnp.where(second < 0, 1, 0)
        out = jnp.where(second < 0, second + 2, second - 6)
        jobs_ref[near] = s + 64 * second + 4096 * first
        jobs_ref[near + 1] = s + SLOTS + 64 * first + 4096 * second
        jobs_ref[LISTS + far] = s + SLOTS + 64 * first + 4096 * out
        jobs_ref[2 * LISTS + down] = s + 64 * out + 4096 * first
        jobs_ref[3 * LISTS + up] = s + 64 * out + 4096 * (first - 6)
        return near + 2 * local, far + 1 - local, down + below, up + 1 - local - below

    for copy in copies:
        copy.wait()
    counted = lax.fori_loop(0, count, listed, (jnp.int32(0),) * 4)
    for kind, (many, spare) in enumerate(zip(counted, (ATOMS, 4, 2, 2))):
        for j in range(8):
            jobs_ref[kind * LISTS + many + j] = 4096 * spare
        jobs_ref[4 * LISTS + kind] = many
    send = pltpu.make_async_copy(jobs_ref, jobs_out, sems.at[3])
    send.start()

    coup = coup_ref[...].astype(F32)
    width = 7 * LANES
    coup = jnp.concatenate([coup, jnp.zeros((SLOTS, width - MODES * SQ), F32)], axis=1)
    lane = iota((SLOTS, LANES), 1)
    for m in range(MODES):
        part = coup if m == 0 else pltpu.roll(coup, width - m * SQ, 1)
        cm[m * SLOTS : (m + 1) * SLOTS, :] = jnp.where(lane < SQ, part[:, :LANES], 0.0)

    ij = iota((LANES, LANES), 0)
    jk = iota((LANES, LANES), 1)
    valid = (ij < SQ) & (jk < SQ)
    row = iota((16, LANES), 0) % NORB
    col = iota((16, LANES), 1)
    sub = iota((8, LANES), 0)

    def expand(keep, other, at):
        spread = jnp.concatenate(
            [
                jnp.where(valid & (other == jk // NORB), 1.0, 0.0),
                jnp.where(valid & (other == jk % NORB), 1.0, 0.0),
            ],
            axis=1,
        ).astype(BF)
        keep = jnp.where(keep == row, 1.0, 0.0)

        def fill(s, carry):
            for m in range(MODES):
                line = cm[pl.ds(m * SLOTS + s, 1), :]
                v[pl.ds(pl.multiple_of(s * (16 * MODES) + m * 16, 16), 16), :] = (
                    jnp.broadcast_to(line, (16, LANES)) * keep
                ).astype(BF)
            return carry

        lax.fori_loop(0, count, fill, 0)
        for part in range(SLOTS // 2):
            lo = part * 32 * MODES
            c12[lo : lo + 32 * MODES, :] = jnp.dot(
                v[lo : lo + 32 * MODES, :], spread, preferred_element_type=F32
            )

        def product(s, carry):
            for m in range(MODES):
                base = pl.multiple_of(s * (16 * MODES) + m * 16, 16)
                first = c12[pl.ds(base, 16), :LANES]
                second = c12[pl.ds(base, 16), LANES:]
                turns = [
                    second[0:8],
                    second[8:16],
                    pltpu.roll(second, 10, 0)[0:8],
                    pltpu.roll(second, 12, 0)[0:8],
                    pltpu.roll(second, 14, 0)[0:8],
                ]
                spreads = [jnp.broadcast_to(first[i : i + 1], (8, LANES)) for i in range(NORB)]
                rows = []
                for g in range(ROWS // 8):
                    lo = 8 * g // NORB
                    hi = min((8 * g + 7) // NORB, NORB - 1)
                    left = spreads[lo]
                    if hi != lo:
                        left = jnp.where(sub < NORB * hi - 8 * g, left, spreads[hi])
                    rows.append(left * turns[g % 5])
                t_ref[at + s, :, m * LANES : (m + 1) * LANES] = jnp.concatenate(rows, axis=0).astype(BF)
            return carry

        lax.fori_loop(0, count, product, 0)

    expand(col // NORB, ij % NORB, 0)
    expand(col % NORB, ij // NORB, SLOTS)

    odd = lax.axis_index("energy") % 2
    e_in = iota((2 * LANES, LANES), 0)
    e_out = iota((2 * LANES, LANES), 1)
    left_first = jnp.where(e_in < 128, e_in, jnp.where(e_in < 192, e_in - 192, e_in - 64))
    right_first = jnp.where(e_in < 128, e_in, jnp.where(e_in < 192, e_in, e_in - 256))
    orders = (jnp.where(odd == 1, left_first, right_first), jnp.where(odd == 1, right_first, left_first))
    for m in range(MODES):
        occ = occ_ref[m]
        step = off_ref[m]
        for which in range(2):
            away = orders[which] - e_out
            s_ref[which, :, m * LANES : (m + 1) * LANES] = jnp.where(
                away == -step, occ, jnp.where(away == step, occ + 1.0, 0.0)
            ).astype(BF)
    send.wait()


def shift_atom(center, halo, s_ref, which, lhs, low, store):
    lhs[0:ROWS, :LANES] = center[0:ROWS]
    lhs[0:ROWS, LANES:] = halo[0:ROWS]
    low[0:ROWS, :LANES] = center[96:SLAB].astype(F32)
    low[0:ROWS, LANES:] = halo[96:SLAB].astype(F32)
    low[ROWS:, :] = jnp.zeros((PITCH - ROWS, 256), F32)
    lhs[PITCH : PITCH + ROWS, :] = low[4 : 4 + ROWS, :].astype(BF)
    for t in range(MODES // 2):
        out = jnp.dot(lhs[...], s_ref[which, :, t * 256 : (t + 1) * 256], preferred_element_type=F32)
        for mm in range(2):
            for r in range(2):
                store(
                    2 * t + mm,
                    r,
                    out[r * PITCH : r * PITCH + ROWS, mm * LANES : (mm + 1) * LANES].astype(BF),
                )


def halo_of(from_a, from_b, x):
    left = iota((SLAB, LANES), 1) < KMAX
    a = from_a[x % 4]
    b = from_b[x % 4]
    return jnp.where(left, a, b) if x < 4 else jnp.where(left, b, a)


def store_in(x_ref, at):
    def store(m, r, value):
        x_ref[at, m * LANES : m * LANES + ROWS, r * LANES : (r + 1) * LANES] = value

    return store


def unfold(total, rows):
    rows[0:ROWS, :] = total[:, :LANES]
    rows[SQ : SQ + ROWS, :] = total[:, LANES:]
    return rows[0:SLAB, :]


class Lists:
    def __init__(self, source, held, sem):
        self.held = held
        self.copy = pltpu.make_async_copy(source, held, sem)
        self.copy.start()

    def ready(self):
        self.copy.wait()
        return self.held


def run_jobs(jobs_ref, kind, chunk, t_ref, x_ref, acc):
    count = jobs_ref[4 * LISTS + kind]

    def step(i, carry):
        for j in range(chunk):
            job = jobs_ref[kind * LISTS + i * chunk + j]
            t, src, dst = job & 63, (job >> 6) & 63, job >> 12
            acc[dst] = acc[dst] + jnp.dot(t_ref[t], x_ref[src], preferred_element_type=F32)
        return carry

    lax.fori_loop(0, (count + chunk - 1) // chunk, step, 0)


def rim_kernel(
    jobs_ref, g_ref, from_b, from_a, s_ref, t_ref, x_old, cross_ref, near_ref, x, part, lhs, low, rows, held, sem
):
    lists = Lists(jobs_ref, held, sem)
    halos = []
    for at, atom in enumerate((0, 1, 6, 7)):
        halos.append(halo_of(from_a, from_b, atom))
        shift_atom(g_ref[atom], halos[at], s_ref, atom // 4, lhs.at[at], low.at[at], store_in(x, atom))
    part[...] = jnp.zeros(part.shape, F32)
    run_jobs(lists.ready(), 1, 4, t_ref, x, part)
    odd = lax.axis_index("atom") % 2

    def fill(ref, side):
        for j in range(2):
            ref[j] = g_ref[6 * side + j]
            ref[2 + j] = halos[2 * side + j]
            ref[4 + j] = unfold(part[2 * side + j], rows.at[2 * side + j]).astype(BF)

    @pl.when(odd == 1)
    def _():
        fill(cross_ref, 1)
        fill(near_ref, 0)

    @pl.when(odd == 0)
    def _():
        fill(cross_ref, 0)
        fill(near_ref, 1)


def early_kernel(
    jobs_ref, g_ref, from_b, from_a, s_ref, t_ref, x_old, cross_old, inner_ref, rim_ref, x, cross_ref, acc, lhs, low, rows, held, sem
):
    @pl.when(lax.axis_index("atom") % 2 == 1)
    def _():
        lists = Lists(jobs_ref, held, sem)
        local_terms(lists, g_ref, from_b, from_a, s_ref, t_ref, inner_ref, rim_ref, x, acc, lhs, low, rows)


def late_kernel(
    jobs_ref, g_ref, from_b, from_a, s_ref, t_ref, x_old, inner_old, rim_old, near_old, inner_ref, rim_ref, x, near_ref, acc, lhs, low, rows, held, sem
):
    @pl.when(lax.axis_index("atom") % 2 == 0)
    def _():
        lists = Lists(jobs_ref, held, sem)
        local_terms(lists, g_ref, from_b, from_a, s_ref, t_ref, inner_ref, rim_ref, x, acc, lhs, low, rows)


def local_terms(lists, g_ref, from_b, from_a, s_ref, t_ref, inner_ref, rim_ref, x, acc, lhs, low, rows):
    for at, atom in enumerate((2, 3, 4, 5)):
        halo = halo_of(from_a, from_b, atom)
        shift_atom(g_ref[atom], halo, s_ref, atom // 4, lhs.at[at], low.at[at], store_in(x, atom))
    acc[...] = jnp.zeros(acc.shape, F32)
    run_jobs(lists.ready(), 0, 8, t_ref, x, acc)
    for j in range(4):
        inner_ref[j] = unfold(acc[2 + j], rows.at[j]).astype(BF)
        rim_ref[j] = acc[j if j < 2 else j + 4]


def final_kernel(
    jobs_ref, cross_ref, near_ref, s_ref, t_ref, rim_ref, inner_ref, x_old, out_ref, x, acc, done, lhs, low, rows, held, sem, sems
):
    lists = Lists(jobs_ref, held, sem)
    odd = lax.axis_index("atom") % 2
    early = pltpu.make_async_copy(inner_ref, out_ref.at[2:6], sems.at[0])
    early.start()
    sides = ((1 - odd, near_ref), (odd, cross_ref))
    for n, (side, ref) in enumerate(sides):
        for j in range(2):
            at = 2 * n + j
            shift_atom(ref[j], ref[2 + j], s_ref, 1 - side, lhs.at[at], low.at[at], store_in(x, 2 * side + j))
            acc[3 * n + j] = rim_ref[2 * side + j]
    held = lists.ready()
    copies = [early]
    for n, (side, ref) in enumerate(sides):
        run_jobs(held, 2 + side, 4, t_ref, x, acc.at[pl.ds(3 * n, 3)])
        for j in range(2):
            at = 2 * n + j
            done[at] = (unfold(acc[3 * n + j], rows.at[at]) + ref[4 + j].astype(F32)).astype(BF)
        copy = pltpu.make_async_copy(done.at[pl.ds(2 * n, 2)], out_ref.at[pl.ds(6 * side, 2)], sems.at[1 + n])
        copy.start()
        copies.append(copy)
    for copy in copies:
        copy.wait()


def swap(value, axis, start):
    count = lax.axis_size(axis)
    pairs = [(i, i + 1) for i in range(start, count - 1, 2)]
    return lax.ppermute(value, axis, pairs + [(b, a) for a, b in pairs])


def call(kernel, outs, scratch, flops, moved, specs, out_specs, aliases={}):
    return pl.pallas_call(
        kernel,
        out_shape=outs,
        in_specs=specs,
        out_specs=out_specs,
        scratch_shapes=scratch,
        input_output_aliases=aliases,
        compiler_params=pltpu.CompilerParams(vmem_limit_bytes=32 * 1024 * 1024),
        cost_estimate=pl.CostEstimate(flops=flops, bytes_accessed=moved, transcendentals=0),
    )


def per_device(green, coupling, pairs, counts, occupation, offsets):
    atoms, slab, e_dev = green.shape
    shape = jax.ShapeDtypeStruct
    dma = pltpu.SemaphoreType.DMA
    pairs = pairs.T

    half = shape((atoms // 2, slab, e_dev), BF)
    taken = (green, coupling, pairs, occupation, offsets)
    to_a, to_b, g, coup, pairs, occ, off = call(
        pack_kernel,
        (half, half) + tuple(shape(v.shape, v.dtype) for v in taken),
        [dma((5,))],
        int(1e6),
        int(1e6),
        [HBM] * 5,
        (VMEM,) * 7,
    )(*[pltpu.with_memory_space_constraint(v, pltpu.HBM) for v in taken])
    from_b = swap(to_b, "energy", 1)
    from_a = swap(to_a, "energy", 0)

    shifted = shape((ATOMS, DEPTH, 256), BF)
    t, s, jobs, x = call(
        build_kernel,
        (shape((2 * SLOTS, ROWS, DEPTH), BF), shape((2, 256, DEPTH), BF), shape((4 * LISTS + 4,), I32), shifted),
        [
            pltpu.VMEM((MODES * SLOTS, LANES), F32),
            pltpu.VMEM((MODES * SLOTS * 16, LANES), BF),
            pltpu.VMEM((MODES * SLOTS * 16, 256), F32),
            pltpu.SMEM((2, SLOTS), I32),
            pltpu.SMEM((MODES,), F32),
            pltpu.SMEM((MODES,), I32),
            pltpu.SMEM((4 * LISTS + 4,), I32),
            dma((4,)),
        ],
        int(3e9),
        int(8e6),
        [SMEM] + [VMEM] * 4,
        (VMEM,) * 4,
    )(counts, pairs, occ, off, coup)

    spare = [
        pltpu.VMEM((4, 2 * PITCH, 256), BF),
        pltpu.VMEM((4, PITCH, 256), F32),
        pltpu.VMEM((4, 208, LANES), F32),
        pltpu.SMEM((4 * LISTS + 4,), I32),
        dma(()),
    ]
    payload = shape((6, slab, e_dev), BF)
    cross, near, x = call(
        rim_kernel,
        (payload, payload, shifted),
        [pltpu.VMEM((5, ROWS, 256), F32)] + spare,
        int(1e9),
        int(1e6),
        [VMEM] * 7,
        (VMEM, VMEM, VMEM),
        {6: 2},
    )(jobs, g, from_b, from_a, s, t, x)
    inner = shape((4, slab, e_dev), BF)
    rim = shape((4, ROWS, 256), F32)
    sums = pltpu.VMEM((9, ROWS, 256), F32)
    inner, rim, x, cross = call(
        early_kernel,
        (inner, rim, shifted, payload),
        [sums] + spare,
        int(3e9),
        int(1e6),
        [VMEM] * 8,
        (VMEM,) * 4,
        {6: 2, 7: 3},
    )(jobs, g, from_b, from_a, s, t, x, cross)
    cross = swap(cross, "atom", 1)
    inner, rim, x, near = call(
        late_kernel,
        (shape(inner.shape, BF), shape(rim.shape, F32), shifted, payload),
        [sums] + spare,
        int(3e9),
        int(1e6),
        [VMEM] * 10,
        (VMEM,) * 4,
        {7: 0, 8: 1, 6: 2, 9: 3},
    )(jobs, g, from_b, from_a, s, t, x, inner, rim, near)
    near = swap(near, "atom", 0)

    return call(
        final_kernel,
        (shape((atoms, slab, e_dev), BF), shifted),
        [pltpu.VMEM((6, ROWS, 256), F32), pltpu.VMEM((4, slab, e_dev), BF)] + spare + [dma((3,))],
        int(1e9),
        int(1e6),
        [VMEM] * 8,
        (HBM, VMEM),
        {7: 1},
    )(jobs, cross, near, s, t, rim, inner, x)[0]


def solution(mesh):
    placed = (P("atom", None, "energy"), P("atom", None), P("atom", None), P("atom"), P(), P())
    return jax.shard_map(
        per_device, mesh=mesh, in_specs=placed, out_specs=P("atom", None, "energy"), check_vma=False
    )
```

```python
import jax
import jax.numpy as jnp
from jax import lax
from jax.experimental import pallas as pl
from jax.experimental.pallas import tpu as pltpu
from jax.sharding import PartitionSpec as P

NORB = 10
MODES = 8
KMAX = 64
SQ = NORB * NORB
ROWS = 104
PITCH = 112
LANES = 128
DEPTH = MODES * LANES
SLOTS = 16
ATOMS = 8
SLAB = 2 * SQ
LISTS = 48
BF = jnp.bfloat16
F32 = jnp.float32
I32 = jnp.int32
VMEM = pl.BlockSpec(memory_space=pltpu.VMEM)
SMEM = pl.BlockSpec(memory_space=pltpu.SMEM)
HBM = pl.BlockSpec(memory_space=pltpu.HBM)


def iota(shape, dim):
    return lax.broadcasted_iota(I32, shape, dim)


def pack_kernel(g_hbm, coup_hbm, pairs_hbm, occ_hbm, off_hbm, to_a, to_b, g, coup, pairs, occ, off, sems):
    half = ATOMS // 2
    moves = ((g_hbm, g), (coup_hbm, coup), (pairs_hbm, pairs), (occ_hbm, occ), (off_hbm, off))
    copies = [pltpu.make_async_copy(src, dst, sems.at[i]) for i, (src, dst) in enumerate(moves)]
    for copy in copies:
        copy.start()
    odd = lax.axis_index("energy") % 2
    pick = (iota((SLAB, LANES), 1) // KMAX) == odd
    copies[0].wait()
    for x in range(half):
        turned = pltpu.roll(g[x + half * odd].astype(F32), KMAX, 1).astype(BF)
        kept = g[x + half - half * odd]
        to_a[x] = jnp.where(pick, turned, kept)
        to_b[x] = jnp.where(pick, kept, turned)
    for copy in copies[1:]:
        copy.wait()


def build_kernel(
    cnt_ref, pairs_in, occ_in, off_in, coup_ref, t_ref, s_ref, jobs_out, x_ref, cm, v, c12, pairs_ref, occ_ref, off_ref, jobs_ref, sems
):
    moves = ((pairs_in, pairs_ref), (occ_in, occ_ref), (off_in, off_ref))
    copies = [pltpu.make_async_copy(src, dst, sems.at[i]) for i, (src, dst) in enumerate(moves)]
    for copy in copies:
        copy.start()
    count = cnt_ref[0]
    base = lax.axis_index("atom") * ATOMS
    for x in range(ATOMS):
        for m in range(MODES):
            x_ref[x, m * LANES + 96 : (m + 1) * LANES, :] = jnp.zeros((32, 256), BF)

    def listed(s, carry):
        near, far, down, up = carry
        first = pairs_ref[0, s] - base
        second = pairs_ref[1, s] - base
        local = jnp.where((second >= 0) & (second < ATOMS), 1, 0)
        below = jnp.where(second < 0, 1, 0)
        out = jnp.where(second < 0, second + 2, second - 6)
        jobs_ref[near] = s + 64 * second + 4096 * first
        jobs_ref[near + 1] = s + SLOTS + 64 * first + 4096 * second
        jobs_ref[LISTS + far] = s + SLOTS + 64 * first + 4096 * out
        jobs_ref[2 * LISTS + down] = s + 64 * out + 4096 * first
        jobs_ref[3 * LISTS + up] = s + 64 * out + 4096 * (first - 6)
        return near + 2 * local, far + 1 - local, down + below, up + 1 - local - below

    for copy in copies:
        copy.wait()
    counted = lax.fori_loop(0, count, listed, (jnp.int32(0),) * 4)
    for kind, (many, spare) in enumerate(zip(counted, (ATOMS, 4, 2, 2))):
        for j in range(8):
            jobs_ref[kind * LISTS + many + j] = 4096 * spare
        jobs_ref[4 * LISTS + kind] = many
    send = pltpu.make_async_copy(jobs_ref, jobs_out, sems.at[3])
    send.start()

    coup = coup_ref[...].astype(F32)
    width = 7 * LANES
    coup = jnp.concatenate([coup, jnp.zeros((SLOTS, width - MODES * SQ), F32)], axis=1)
    lane = iota((SLOTS, LANES), 1)
    for m in range(MODES):
        part = coup if m == 0 else pltpu.roll(coup, width - m * SQ, 1)
        cm[m * SLOTS : (m + 1) * SLOTS, :] = jnp.where(lane < SQ, part[:, :LANES], 0.0)

    ij = iota((LANES, LANES), 0)
    jk = iota((LANES, LANES), 1)
    valid = (ij < SQ) & (jk < SQ)
    row = iota((16, LANES), 0) % NORB
    col = iota((16, LANES), 1)
    sub = iota((8, LANES), 0)

    def expand(keep, other, at):
        spread = jnp.concatenate(
            [
                jnp.where(valid & (other == jk // NORB), 1.0, 0.0),
                jnp.where(valid & (other == jk % NORB), 1.0, 0.0),
            ],
            axis=1,
        ).astype(BF)
        keep = jnp.where(keep == row, 1.0, 0.0)

        def fill(s, carry):
            for m in range(MODES):
                line = cm[pl.ds(m * SLOTS + s, 1), :]
                v[pl.ds(pl.multiple_of(s * (16 * MODES) + m * 16, 16), 16), :] = (
                    jnp.broadcast_to(line, (16, LANES)) * keep
                ).astype(BF)
            return carry

        lax.fori_loop(0, count, fill, 0)
        for part in range(SLOTS // 2):
            lo = part * 32 * MODES
            c12[lo : lo + 32 * MODES, :] = jnp.dot(
                v[lo : lo + 32 * MODES, :], spread, preferred_element_type=F32
            )

        def product(s, carry):
            for m in range(MODES):
                base = pl.multiple_of(s * (16 * MODES) + m * 16, 16)
                first = c12[pl.ds(base, 16), :LANES]
                second = c12[pl.ds(base, 16), LANES:]
                turns = [
                    second[0:8],
                    second[8:16],
                    pltpu.roll(second, 10, 0)[0:8],
                    pltpu.roll(second, 12, 0)[0:8],
                    pltpu.roll(second, 14, 0)[0:8],
                ]
                spreads = [jnp.broadcast_to(first[i : i + 1], (8, LANES)) for i in range(NORB)]
                rows = []
                for g in range(ROWS // 8):
                    lo = 8 * g // NORB
                    hi = min((8 * g + 7) // NORB, NORB - 1)
                    left = spreads[lo]
                    if hi != lo:
                        left = jnp.where(sub < NORB * hi - 8 * g, left, spreads[hi])
                    rows.append(left * turns[g % 5])
                t_ref[at + s, :, m * LANES : (m + 1) * LANES] = jnp.concatenate(rows, axis=0).astype(BF)
            return carry

        lax.fori_loop(0, count, product, 0)

    expand(col // NORB, ij % NORB, 0)
    expand(col % NORB, ij // NORB, SLOTS)

    odd = lax.axis_index("energy") % 2
    e_in = iota((2 * LANES, LANES), 0)
    e_out = iota((2 * LANES, LANES), 1)
    left_first = jnp.where(e_in < 128, e_in, jnp.where(e_in < 192, e_in - 192, e_in - 64))
    right_first = jnp.where(e_in < 128, e_in, jnp.where(e_in < 192, e_in, e_in - 256))
    orders = (jnp.where(odd == 1, left_first, right_first), jnp.where(odd == 1, right_first, left_first))
    for m in range(MODES):
        occ = occ_ref[m]
        step = off_ref[m]
        for which in range(2):
            away = orders[which] - e_out
            s_ref[which, :, m * LANES : (m + 1) * LANES] = jnp.where(
                away == -step, occ, jnp.where(away == step, occ + 1.0, 0.0)
            ).astype(BF)
    send.wait()


def shift_atom(center, halo, s_ref, which, lhs, low, store):
    lhs[0:ROWS, :LANES] = center[0:ROWS]
    lhs[0:ROWS, LANES:] = halo[0:ROWS]
    low[0:ROWS, :LANES] = center[96:SLAB].astype(F32)
    low[0:ROWS, LANES:] = halo[96:SLAB].astype(F32)
    low[ROWS:, :] = jnp.zeros((PITCH - ROWS, 256), F32)
    lhs[PITCH : PITCH + ROWS, :] = low[4 : 4 + ROWS, :].astype(BF)
    for t in range(MODES // 2):
        out = jnp.dot(lhs[...], s_ref[which, :, t * 256 : (t + 1) * 256], preferred_element_type=F32)
        for mm in range(2):
            for r in range(2):
                store(
                    2 * t + mm,
                    r,
                    out[r * PITCH : r * PITCH + ROWS, mm * LANES : (mm + 1) * LANES].astype(BF),
                )


def halo_of(from_a, from_b, x):
    left = iota((SLAB, LANES), 1) < KMAX
    a = from_a[x % 4]
    b = from_b[x % 4]
    return jnp.where(left, a, b) if x < 4 else jnp.where(left, b, a)


def store_in(x_ref, at):
    def store(m, r, value):
        x_ref[at, m * LANES : m * LANES + ROWS, r * LANES : (r + 1) * LANES] = value

    return store


def unfold(total, rows):
    rows[0:ROWS, :] = total[:, :LANES]
    rows[SQ : SQ + ROWS, :] = total[:, LANES:]
    return rows[0:SLAB, :]


class Lists:
    def __init__(self, source, held, sem):
        self.held = held
        self.copy = pltpu.make_async_copy(source, held, sem)
        self.copy.start()

    def ready(self):
        self.copy.wait()
        return self.held


def run_jobs(jobs_ref, kind, chunk, t_ref, x_ref, acc):
    count = jobs_ref[4 * LISTS + kind]

    def step(i, carry):
        for j in range(chunk):
            job = jobs_ref[kind * LISTS + i * chunk + j]
            t, src, dst = job & 63, (job >> 6) & 63, job >> 12
            acc[dst] = acc[dst] + jnp.dot(t_ref[t], x_ref[src], preferred_element_type=F32)
        return carry

    lax.fori_loop(0, (count + chunk - 1) // chunk, step, 0)


def rim_kernel(
    jobs_ref, g_ref, from_b, from_a, s_ref, t_ref, x_old, cross_ref, near_ref, x, part, lhs, low, rows, held, sem
):
    lists = Lists(jobs_ref, held, sem)
    halos = []
    for at, atom in enumerate((0, 1, 6, 7)):
        halos.append(halo_of(from_a, from_b, atom))
        shift_atom(g_ref[atom], halos[at], s_ref, atom // 4, lhs.at[at], low.at[at], store_in(x, atom))
    part[...] = jnp.zeros(part.shape, F32)
    run_jobs(lists.ready(), 1, 4, t_ref, x, part)
    odd = lax.axis_index("atom") % 2

    def fill(ref, side):
        for j in range(2):
            ref[j] = g_ref[6 * side + j]
            ref[2 + j] = halos[2 * side + j]
            ref[4 + j] = unfold(part[2 * side + j], rows.at[2 * side + j]).astype(BF)

    @pl.when(odd == 1)
    def _():
        fill(cross_ref, 1)
        fill(near_ref, 0)

    @pl.when(odd == 0)
    def _():
        fill(cross_ref, 0)
        fill(near_ref, 1)


def local_kernel(
    jobs_ref, g_ref, from_b, from_a, s_ref, t_ref, x_old, inner_ref, rim_ref, x, acc, lhs, low, rows, held, sem
):
    lists = Lists(jobs_ref, held, sem)
    for at, atom in enumerate((2, 3, 4, 5)):
        halo = halo_of(from_a, from_b, atom)
        shift_atom(g_ref[atom], halo, s_ref, atom // 4, lhs.at[at], low.at[at], store_in(x, atom))
    acc[...] = jnp.zeros(acc.shape, F32)
    run_jobs(lists.ready(), 0, 8, t_ref, x, acc)
    for j in range(4):
        inner_ref[j] = unfold(acc[2 + j], rows.at[j]).astype(BF)
        rim_ref[j] = acc[j if j < 2 else j + 4]


def final_kernel(
    jobs_ref, cross_ref, near_ref, s_ref, t_ref, rim_ref, inner_ref, x_old, out_ref, x, acc, done, lhs, low, rows, held, sem, sems
):
    lists = Lists(jobs_ref, held, sem)
    odd = lax.axis_index("atom") % 2
    early = pltpu.make_async_copy(inner_ref, out_ref.at[2:6], sems.at[0])
    early.start()
    sides = ((1 - odd, near_ref), (odd, cross_ref))
    for n, (side, ref) in enumerate(sides):
        for j in range(2):
            at = 2 * n + j
            shift_atom(ref[j], ref[2 + j], s_ref, 1 - side, lhs.at[at], low.at[at], store_in(x, 2 * side + j))
            acc[3 * n + j] = rim_ref[2 * side + j]
    held = lists.ready()
    copies = [early]
    for n, (side, ref) in enumerate(sides):
        run_jobs(held, 2 + side, 4, t_ref, x, acc.at[pl.ds(3 * n, 3)])
        for j in range(2):
            at = 2 * n + j
            done[at] = (unfold(acc[3 * n + j], rows.at[at]) + ref[4 + j].astype(F32)).astype(BF)
        copy = pltpu.make_async_copy(done.at[pl.ds(2 * n, 2)], out_ref.at[pl.ds(6 * side, 2)], sems.at[1 + n])
        copy.start()
        copies.append(copy)
    for copy in copies:
        copy.wait()


def swap(value, axis, start):
    count = lax.axis_size(axis)
    pairs = [(i, i + 1) for i in range(start, count - 1, 2)]
    return lax.ppermute(value, axis, pairs + [(b, a) for a, b in pairs])


def call(kernel, outs, scratch, flops, moved, specs, out_specs, aliases={}):
    return pl.pallas_call(
        kernel,
        out_shape=outs,
        in_specs=specs,
        out_specs=out_specs,
        scratch_shapes=scratch,
        input_output_aliases=aliases,
        compiler_params=pltpu.CompilerParams(vmem_limit_bytes=32 * 1024 * 1024),
        cost_estimate=pl.CostEstimate(flops=flops, bytes_accessed=moved, transcendentals=0),
    )


def per_device(green, coupling, pairs, counts, occupation, offsets):
    atoms, slab, e_dev = green.shape
    shape = jax.ShapeDtypeStruct
    dma = pltpu.SemaphoreType.DMA
    pairs = pairs.T

    half = shape((atoms // 2, slab, e_dev), BF)
    taken = (green, coupling, pairs, occupation, offsets)
    to_a, to_b, g, coup, pairs, occ, off = call(
        pack_kernel,
        (half, half) + tuple(shape(v.shape, v.dtype) for v in taken),
        [dma((5,))],
        int(1e6),
        int(1e6),
        [HBM] * 5,
        (VMEM,) * 7,
    )(*[pltpu.with_memory_space_constraint(v, pltpu.HBM) for v in taken])
    from_b = swap(to_b, "energy", 1)
    from_a = swap(to_a, "energy", 0)

    shifted = shape((ATOMS, DEPTH, 256), BF)
    t, s, jobs, x = call(
        build_kernel,
        (shape((2 * SLOTS, ROWS, DEPTH), BF), shape((2, 256, DEPTH), BF), shape((4 * LISTS + 4,), I32), shifted),
        [
            pltpu.VMEM((MODES * SLOTS, LANES), F32),
            pltpu.VMEM((MODES * SLOTS * 16, LANES), BF),
            pltpu.VMEM((MODES * SLOTS * 16, 256), F32),
            pltpu.SMEM((2, SLOTS), I32),
            pltpu.SMEM((MODES,), F32),
            pltpu.SMEM((MODES,), I32),
            pltpu.SMEM((4 * LISTS + 4,), I32),
            dma((4,)),
        ],
        int(3e9),
        int(8e6),
        [SMEM] + [VMEM] * 4,
        (VMEM,) * 4,
    )(counts, pairs, occ, off, coup)

    spare = [
        pltpu.VMEM((4, 2 * PITCH, 256), BF),
        pltpu.VMEM((4, PITCH, 256), F32),
        pltpu.VMEM((4, 208, LANES), F32),
        pltpu.SMEM((4 * LISTS + 4,), I32),
        dma(()),
    ]
    payload = shape((6, slab, e_dev), BF)
    cross, near, x = call(
        rim_kernel,
        (payload, payload, shifted),
        [pltpu.VMEM((5, ROWS, 256), F32)] + spare,
        int(1e9),
        int(1e6),
        [VMEM] * 7,
        (VMEM, VMEM, VMEM),
        {6: 2},
    )(jobs, g, from_b, from_a, s, t, x)
    cross = swap(cross, "atom", 1)
    near = swap(near, "atom", 0)
    inner, rim, x = call(
        local_kernel,
        (shape((4, slab, e_dev), BF), shape((4, ROWS, 256), F32), shifted),
        [pltpu.VMEM((9, ROWS, 256), F32)] + spare,
        int(3e9),
        int(1e6),
        [VMEM] * 7,
        (VMEM,) * 3,
        {6: 2},
    )(jobs, g, from_b, from_a, s, t, x)

    return call(
        final_kernel,
        (shape((atoms, slab, e_dev), BF), shifted),
        [pltpu.VMEM((6, ROWS, 256), F32), pltpu.VMEM((4, slab, e_dev), BF)] + spare + [dma((3,))],
        int(1e9),
        int(1e6),
        [VMEM] * 8,
        (HBM, VMEM),
        {7: 1},
    )(jobs, cross, near, s, t, rim, inner, x)[0]


def solution(mesh):
    placed = (P("atom", None, "energy"), P("atom", None), P("atom", None), P("atom"), P(), P())
    return jax.shard_map(
        per_device, mesh=mesh, in_specs=placed, out_specs=P("atom", None, "energy"), check_vma=False
    )
```

```python
import jax
import jax.numpy as jnp
from jax import lax
from jax.experimental import pallas as pl
from jax.experimental.pallas import tpu as pltpu
from jax.sharding import PartitionSpec as P

NORB = 10
MODES = 8
KMAX = 64
SQ = NORB * NORB
ROWS = 104
PITCH = 112
LANES = 128
DEPTH = MODES * LANES
SLOTS = 16
ATOMS = 8
SLAB = 2 * SQ
LISTS = 48
BF = jnp.bfloat16
F32 = jnp.float32
I32 = jnp.int32
VMEM = pl.BlockSpec(memory_space=pltpu.VMEM)
SMEM = pl.BlockSpec(memory_space=pltpu.SMEM)
HBM = pl.BlockSpec(memory_space=pltpu.HBM)


def iota(shape, dim):
    return lax.broadcasted_iota(I32, shape, dim)


def pack_kernel(g_hbm, coup_hbm, pairs_hbm, occ_hbm, off_hbm, first, second, g, coup, pairs, occ, off, sems):
    half = ATOMS // 2
    moves = ((g_hbm, g), (coup_hbm, coup), (pairs_hbm, pairs), (occ_hbm, occ), (off_hbm, off))
    copies = [pltpu.make_async_copy(src, dst, sems.at[i]) for i, (src, dst) in enumerate(moves)]
    for copy in copies:
        copy.start()
    odd = lax.axis_index("energy") % 2
    pick = (iota((SLAB, LANES), 1) // KMAX) == (odd + 1 + lax.axis_index("atom")) % 2
    copies[0].wait()
    for x in range(half):
        turned = pltpu.roll(g[x + half * odd].astype(F32), KMAX, 1).astype(BF)
        kept = g[x + half - half * odd]
        first[x] = jnp.where(pick, turned, kept)
        second[x] = jnp.where(pick, kept, turned)
    for copy in copies[1:]:
        copy.wait()


def build_kernel(
    cnt_ref, pairs_in, occ_in, off_in, coup_ref, t_ref, s_ref, jobs_out, x_ref, cm, v, c12, pairs_ref, occ_ref, off_ref, jobs_ref, sems
):
    moves = ((pairs_in, pairs_ref), (occ_in, occ_ref), (off_in, off_ref))
    copies = [pltpu.make_async_copy(src, dst, sems.at[i]) for i, (src, dst) in enumerate(moves)]
    for copy in copies:
        copy.start()
    count = cnt_ref[0]
    base = lax.axis_index("atom") * ATOMS
    for x in range(ATOMS):
        for m in range(MODES):
            x_ref[x, m * LANES + 96 : (m + 1) * LANES, :] = jnp.zeros((32, 256), BF)

    def listed(s, carry):
        near, far, down, up = carry
        first = pairs_ref[0, s] - base
        second = pairs_ref[1, s] - base
        local = jnp.where((second >= 0) & (second < ATOMS), 1, 0)
        below = jnp.where(second < 0, 1, 0)
        out = jnp.where(second < 0, second + 2, second - 6)
        jobs_ref[near] = s + 64 * second + 4096 * first
        jobs_ref[near + 1] = s + SLOTS + 64 * first + 4096 * second
        jobs_ref[LISTS + far] = s + SLOTS + 64 * first + 4096 * out
        jobs_ref[2 * LISTS + down] = s + 64 * out + 4096 * first
        jobs_ref[3 * LISTS + up] = s + 64 * out + 4096 * (first - 6)
        return near + 2 * local, far + 1 - local, down + below, up + 1 - local - below

    for copy in copies:
        copy.wait()
    counted = lax.fori_loop(0, count, listed, (jnp.int32(0),) * 4)
    for kind, (many, spare) in enumerate(zip(counted, (ATOMS, 4, 2, 2))):
        for j in range(8):
            jobs_ref[kind * LISTS + many + j] = 4096 * spare
        jobs_ref[4 * LISTS + kind] = many
    send = pltpu.make_async_copy(jobs_ref, jobs_out, sems.at[3])
    send.start()

    coup = coup_ref[...].astype(F32)
    width = 7 * LANES
    coup = jnp.concatenate([coup, jnp.zeros((SLOTS, width - MODES * SQ), F32)], axis=1)
    lane = iota((SLOTS, LANES), 1)
    for m in range(MODES):
        part = coup if m == 0 else pltpu.roll(coup, width - m * SQ, 1)
        cm[m * SLOTS : (m + 1) * SLOTS, :] = jnp.where(lane < SQ, part[:, :LANES], 0.0)

    ij = iota((LANES, LANES), 0)
    jk = iota((LANES, LANES), 1)
    valid = (ij < SQ) & (jk < SQ)
    row = iota((16, LANES), 0) % NORB
    col = iota((16, LANES), 1)
    sub = iota((8, LANES), 0)

    def expand(keep, other, at):
        spread = jnp.concatenate(
            [
                jnp.where(valid & (other == jk // NORB), 1.0, 0.0),
                jnp.where(valid & (other == jk % NORB), 1.0, 0.0),
            ],
            axis=1,
        ).astype(BF)
        keep = jnp.where(keep == row, 1.0, 0.0)

        def fill(s, carry):
            for m in range(MODES):
                line = cm[pl.ds(m * SLOTS + s, 1), :]
                v[pl.ds(pl.multiple_of(s * (16 * MODES) + m * 16, 16), 16), :] = (
                    jnp.broadcast_to(line, (16, LANES)) * keep
                ).astype(BF)
            return carry

        lax.fori_loop(0, count, fill, 0)
        for part in range(SLOTS // 2):
            lo = part * 32 * MODES
            c12[lo : lo + 32 * MODES, :] = jnp.dot(
                v[lo : lo + 32 * MODES, :], spread, preferred_element_type=F32
            )

        def product(s, carry):
            for m in range(MODES):
                base = pl.multiple_of(s * (16 * MODES) + m * 16, 16)
                first = c12[pl.ds(base, 16), :LANES]
                second = c12[pl.ds(base, 16), LANES:]
                turns = [
                    second[0:8],
                    second[8:16],
                    pltpu.roll(second, 10, 0)[0:8],
                    pltpu.roll(second, 12, 0)[0:8],
                    pltpu.roll(second, 14, 0)[0:8],
                ]
                spreads = [jnp.broadcast_to(first[i : i + 1], (8, LANES)) for i in range(NORB)]
                rows = []
                for g in range(ROWS // 8):
                    lo = 8 * g // NORB
                    hi = min((8 * g + 7) // NORB, NORB - 1)
                    left = spreads[lo]
                    if hi != lo:
                        left = jnp.where(sub < NORB * hi - 8 * g, left, spreads[hi])
                    rows.append(left * turns[g % 5])
                t_ref[at + s, :, m * LANES : (m + 1) * LANES] = jnp.concatenate(rows, axis=0).astype(BF)
            return carry

        lax.fori_loop(0, count, product, 0)

    expand(col // NORB, ij % NORB, 0)
    expand(col % NORB, ij // NORB, SLOTS)

    odd = lax.axis_index("energy") % 2
    e_in = iota((2 * LANES, LANES), 0)
    e_out = iota((2 * LANES, LANES), 1)
    away = jnp.where(e_in < 128, e_in, jnp.where(e_in < 192, e_in - 192, e_in - 64)) - e_out
    for m in range(MODES):
        occ = occ_ref[m]
        step = off_ref[m]
        band = jnp.where(away == -step, occ, jnp.where(away == step, occ + 1.0, 0.0)).astype(BF)
        cols = slice(m * LANES, (m + 1) * LANES)
        s_ref[1 - odd, :, cols] = band
        s_ref[odd, 0:128, cols] = band[0:128]
        s_ref[odd, 128:192, cols] = band[192:256]
        s_ref[odd, 192:256, cols] = band[128:192]
    send.wait()


def shift_atom(center, halo, s_ref, which, lhs, low, store):
    lhs[0:ROWS, :LANES] = center[0:ROWS]
    lhs[0:ROWS, LANES:] = halo[0:ROWS]
    low[0:ROWS, :LANES] = center[96:SLAB].astype(F32)
    low[0:ROWS, LANES:] = halo[96:SLAB].astype(F32)
    low[ROWS:, :] = jnp.zeros((PITCH - ROWS, 256), F32)
    lhs[PITCH : PITCH + ROWS, :] = low[4 : 4 + ROWS, :].astype(BF)
    for t in range(MODES // 2):
        out = jnp.dot(lhs[...], s_ref[which, :, t * 256 : (t + 1) * 256], preferred_element_type=F32)
        for mm in range(2):
            for r in range(2):
                store(
                    2 * t + mm,
                    r,
                    out[r * PITCH : r * PITCH + ROWS, mm * LANES : (mm + 1) * LANES].astype(BF),
                )


def halo_of(first, second, x):
    pick = iota((SLAB, LANES), 1) // KMAX == 1 - lax.axis_index("atom") % 2
    a = first[x % 4]
    b = second[x % 4]
    return jnp.where(pick, a, b) if x < 4 else jnp.where(pick, b, a)


def store_in(x_ref, at):
    def store(m, r, value):
        x_ref[at, m * LANES : m * LANES + ROWS, r * LANES : (r + 1) * LANES] = value

    return store


def unfold(total, rows):
    rows[0:ROWS, :] = total[:, :LANES]
    rows[SQ : SQ + ROWS, :] = total[:, LANES:]
    return rows[0:SLAB, :]


class Lists:
    def __init__(self, source, held, sem):
        self.held = held
        self.copy = pltpu.make_async_copy(source, held, sem)
        self.copy.start()

    def ready(self):
        self.copy.wait()
        return self.held


def run_jobs(jobs_ref, kind, chunk, t_ref, x_ref, acc):
    count = jobs_ref[4 * LISTS + kind]

    def step(i, carry):
        for j in range(chunk):
            job = jobs_ref[kind * LISTS + i * chunk + j]
            t, src, dst = job & 63, (job >> 6) & 63, job >> 12
            acc[dst] = acc[dst] + jnp.dot(t_ref[t], x_ref[src], preferred_element_type=F32)
        return carry

    lax.fori_loop(0, (count + chunk - 1) // chunk, step, 0)


def rim_kernel(
    jobs_ref, g_ref, first, second, s_ref, t_ref, x_old, cross_ref, near_ref, x, part, lhs, low, rows, held, sem
):
    lists = Lists(jobs_ref, held, sem)
    halos = []
    for at, atom in enumerate((0, 1, 6, 7)):
        halos.append(halo_of(first, second, atom))
        shift_atom(g_ref[atom], halos[at], s_ref, atom // 4, lhs.at[at], low.at[at], store_in(x, atom))
    part[...] = jnp.zeros(part.shape, F32)
    run_jobs(lists.ready(), 1, 4, t_ref, x, part)
    odd = lax.axis_index("atom") % 2

    def fill(ref, side):
        for j in range(2):
            ref[j] = g_ref[6 * side + j]
            ref[2 + j] = halos[2 * side + j]
            ref[4 + j] = unfold(part[2 * side + j], rows.at[2 * side + j]).astype(BF)

    @pl.when(odd == 1)
    def _():
        fill(cross_ref, 1)
        fill(near_ref, 0)

    @pl.when(odd == 0)
    def _():
        fill(cross_ref, 0)
        fill(near_ref, 1)


def local_kernel(
    jobs_ref, g_ref, first, second, s_ref, t_ref, x_old, inner_ref, rim_ref, x, acc, lhs, low, rows, held, sem
):
    lists = Lists(jobs_ref, held, sem)
    for at, atom in enumerate((2, 3, 4, 5)):
        halo = halo_of(first, second, atom)
        shift_atom(g_ref[atom], halo, s_ref, atom // 4, lhs.at[at], low.at[at], store_in(x, atom))
    acc[...] = jnp.zeros(acc.shape, F32)
    run_jobs(lists.ready(), 0, 8, t_ref, x, acc)
    for j in range(4):
        inner_ref[j] = unfold(acc[2 + j], rows.at[j]).astype(BF)
        rim_ref[j] = acc[j if j < 2 else j + 4]


def final_kernel(
    jobs_ref, cross_ref, near_ref, s_ref, t_ref, rim_ref, inner_ref, x_old, out_ref, x, acc, done, lhs, low, rows, held, sem, sems
):
    lists = Lists(jobs_ref, held, sem)
    odd = lax.axis_index("atom") % 2
    early = pltpu.make_async_copy(inner_ref, out_ref.at[2:6], sems.at[0])
    early.start()
    sides = ((1 - odd, near_ref), (odd, cross_ref))
    for n, (side, ref) in enumerate(sides):
        for j in range(2):
            at = 2 * n + j
            shift_atom(ref[j], ref[2 + j], s_ref, 1 - side, lhs.at[at], low.at[at], store_in(x, 2 * side + j))
            acc[3 * n + j] = rim_ref[2 * side + j]
    held = lists.ready()
    copies = [early]
    for n, (side, ref) in enumerate(sides):
        run_jobs(held, 2 + side, 4, t_ref, x, acc.at[pl.ds(3 * n, 3)])
        for j in range(2):
            at = 2 * n + j
            done[at] = (unfold(acc[3 * n + j], rows.at[at]) + ref[4 + j].astype(F32)).astype(BF)
        copy = pltpu.make_async_copy(done.at[pl.ds(2 * n, 2)], out_ref.at[pl.ds(6 * side, 2)], sems.at[1 + n])
        copy.start()
        copies.append(copy)
    for copy in copies:
        copy.wait()


def swap(value, axis, start):
    count = lax.axis_size(axis)
    pairs = [(i, i + 1) for i in range(start, count - 1, 2)]
    return lax.ppermute(value, axis, pairs + [(b, a) for a, b in pairs])


def mixed_swap(value, start):
    parts, count = lax.axis_size("atom"), lax.axis_size("energy")
    pairs = []
    for part in range(parts):
        for i in range((start + part) % 2, count - 1, 2):
            pairs.append((part * count + i, part * count + i + 1))
    return lax.ppermute(value, ("atom", "energy"), pairs + [(b, a) for a, b in pairs])


def call(kernel, outs, scratch, flops, moved, specs, out_specs, aliases={}):
    return pl.pallas_call(
        kernel,
        out_shape=outs,
        in_specs=specs,
        out_specs=out_specs,
        scratch_shapes=scratch,
        input_output_aliases=aliases,
        compiler_params=pltpu.CompilerParams(vmem_limit_bytes=32 * 1024 * 1024),
        cost_estimate=pl.CostEstimate(flops=flops, bytes_accessed=moved, transcendentals=0),
    )


def per_device(green, coupling, pairs, counts, occupation, offsets):
    atoms, slab, e_dev = green.shape
    shape = jax.ShapeDtypeStruct
    dma = pltpu.SemaphoreType.DMA
    pairs = pairs.T

    half = shape((atoms // 2, slab, e_dev), BF)
    taken = (green, coupling, pairs, occupation, offsets)
    first, second, g, coup, pairs, occ, off = call(
        pack_kernel,
        (half, half) + tuple(shape(v.shape, v.dtype) for v in taken),
        [dma((5,))],
        int(1e6),
        int(1e6),
        [HBM] * 5,
        (VMEM,) * 7,
    )(*[pltpu.with_memory_space_constraint(v, pltpu.HBM) for v in taken])
    first = mixed_swap(first, 1)
    second = mixed_swap(second, 0)

    shifted = shape((ATOMS, DEPTH, 256), BF)
    t, s, jobs, x = call(
        build_kernel,
        (shape((2 * SLOTS, ROWS, DEPTH), BF), shape((2, 256, DEPTH), BF), shape((4 * LISTS + 4,), I32), shifted),
        [
            pltpu.VMEM((MODES * SLOTS, LANES), F32),
            pltpu.VMEM((MODES * SLOTS * 16, LANES), BF),
            pltpu.VMEM((MODES * SLOTS * 16, 256), F32),
            pltpu.SMEM((2, SLOTS), I32),
            pltpu.SMEM((MODES,), F32),
            pltpu.SMEM((MODES,), I32),
            pltpu.SMEM((4 * LISTS + 4,), I32),
            dma((4,)),
        ],
        int(3e9),
        int(8e6),
        [SMEM] + [VMEM] * 4,
        (VMEM,) * 4,
    )(counts, pairs, occ, off, coup)

    spare = [
        pltpu.VMEM((4, 2 * PITCH, 256), BF),
        pltpu.VMEM((4, PITCH, 256), F32),
        pltpu.VMEM((4, 208, LANES), F32),
        pltpu.SMEM((4 * LISTS + 4,), I32),
        dma(()),
    ]
    payload = shape((6, slab, e_dev), BF)
    cross, near, x = call(
        rim_kernel,
        (payload, payload, shifted),
        [pltpu.VMEM((5, ROWS, 256), F32)] + spare,
        int(1e9),
        int(1e6),
        [VMEM] * 7,
        (VMEM, VMEM, VMEM),
        {6: 2},
    )(jobs, g, first, second, s, t, x)
    cross = swap(cross, "atom", 1)
    near = swap(near, "atom", 0)
    inner, rim, x = call(
        local_kernel,
        (shape((4, slab, e_dev), BF), shape((4, ROWS, 256), F32), shifted),
        [pltpu.VMEM((9, ROWS, 256), F32)] + spare,
        int(3e9),
        int(1e6),
        [VMEM] * 7,
        (VMEM,) * 3,
        {6: 2},
    )(jobs, g, first, second, s, t, x)

    return call(
        final_kernel,
        (shape((atoms, slab, e_dev), BF), shifted),
        [pltpu.VMEM((6, ROWS, 256), F32), pltpu.VMEM((4, slab, e_dev), BF)] + spare + [dma((3,))],
        int(1e9),
        int(1e6),
        [VMEM] * 8,
        (HBM, VMEM),
        {7: 1},
    )(jobs, cross, near, s, t, rim, inner, x)[0]


def solution(mesh):
    placed = (P("atom", None, "energy"), P("atom", None), P("atom", None), P("atom"), P(), P())
    return jax.shard_map(
        per_device, mesh=mesh, in_specs=placed, out_specs=P("atom", None, "energy"), check_vma=False
    )
```

```python
import functools

import jax
import jax.numpy as jnp
from jax import lax
from jax.experimental import pallas as pl
from jax.experimental.pallas import tpu as pltpu
from jax.sharding import PartitionSpec as P

NORB = 10
MODES = 8
KMAX = 64
SQ = NORB * NORB
ROWS = 104
PITCH = 112
LANES = 128
DEPTH = MODES * LANES
SLOTS = 16
ATOMS = 8
SLAB = 2 * SQ
LISTS = 48
BF = jnp.bfloat16
F32 = jnp.float32
I32 = jnp.int32
VMEM = pl.BlockSpec(memory_space=pltpu.VMEM)
SMEM = pl.BlockSpec(memory_space=pltpu.SMEM)
HBM = pl.BlockSpec(memory_space=pltpu.HBM)


def iota(shape, dim):
    return lax.broadcasted_iota(I32, shape, dim)


def pack_kernel(g_hbm, coup_hbm, pairs_hbm, occ_hbm, off_hbm, first, second, g, coup, pairs, occ, off, sems):
    half = ATOMS // 2
    moves = ((g_hbm, g), (coup_hbm, coup), (pairs_hbm, pairs), (occ_hbm, occ), (off_hbm, off))
    copies = [pltpu.make_async_copy(src, dst, sems.at[i]) for i, (src, dst) in enumerate(moves)]
    for copy in copies:
        copy.start()
    odd = lax.axis_index("energy") % 2
    pick = (iota((SLAB, LANES), 1) // KMAX) == (odd + 1 + lax.axis_index("atom")) % 2
    copies[0].wait()
    for x in range(half):
        turned = pltpu.roll(g[x + half * odd].astype(F32), KMAX, 1).astype(BF)
        kept = g[x + half - half * odd]
        first[x] = jnp.where(pick, turned, kept)
        second[x] = jnp.where(pick, kept, turned)
    for copy in copies[1:]:
        copy.wait()


def build_kernel(
    cnt_ref, pairs_in, occ_in, off_in, coup_ref, t_ref, s_ref, jobs_out, x_ref, cm, v, c12, pairs_ref, occ_ref, off_ref, jobs_ref, sems
):
    moves = ((pairs_in, pairs_ref), (occ_in, occ_ref), (off_in, off_ref))
    copies = [pltpu.make_async_copy(src, dst, sems.at[i]) for i, (src, dst) in enumerate(moves)]
    for copy in copies:
        copy.start()
    count = cnt_ref[0]
    base = lax.axis_index("atom") * ATOMS
    for x in range(ATOMS):
        for m in range(MODES):
            x_ref[x, m * LANES + 96 : (m + 1) * LANES, :] = jnp.zeros((32, 256), BF)

    def listed(s, carry):
        near, down, up, far = carry
        first = pairs_ref[0, s] - base
        second = pairs_ref[1, s] - base
        local = jnp.where((second >= 0) & (second < ATOMS), 1, 0)
        below = jnp.where(second < 0, 1, 0)
        above = 1 - local - below
        jobs_ref[near] = s + 64 * second + 4096 * first
        jobs_ref[near + 1] = s + SLOTS + 64 * first + 4096 * second
        jobs_ref[LISTS + down] = s + SLOTS + 64 * first + 4096 * (second + 2)
        jobs_ref[2 * LISTS + up] = s + SLOTS + 64 * first + 4096 * (second - ATOMS)
        jobs_ref[3 * LISTS + far] = s + 64 * (second + 2 - 8 * above) + 4096 * (first - 4 * above)
        return near + 2 * local, down + below, up + above, far + 1 - local

    for copy in copies:
        copy.wait()
    counted = lax.fori_loop(0, count, listed, (jnp.int32(0),) * 4)
    for kind, (many, spare) in enumerate(zip(counted, (ATOMS, 2, 2, 4))):
        for j in range(8):
            jobs_ref[kind * LISTS + many + j] = 4096 * spare
        jobs_ref[4 * LISTS + kind] = many
    send = pltpu.make_async_copy(jobs_ref, jobs_out, sems.at[3])
    send.start()

    coup = coup_ref[...].astype(F32)
    width = 7 * LANES
    coup = jnp.concatenate([coup, jnp.zeros((SLOTS, width - MODES * SQ), F32)], axis=1)
    lane = iota((SLOTS, LANES), 1)
    for m in range(MODES):
        part = coup if m == 0 else pltpu.roll(coup, width - m * SQ, 1)
        cm[m * SLOTS : (m + 1) * SLOTS, :] = jnp.where(lane < SQ, part[:, :LANES], 0.0)

    ij = iota((LANES, LANES), 0)
    jk = iota((LANES, LANES), 1)
    valid = (ij < SQ) & (jk < SQ)
    row = iota((16, LANES), 0) % NORB
    col = iota((16, LANES), 1)
    sub = iota((8, LANES), 0)

    def expand(keep, other, at):
        spread = jnp.concatenate(
            [
                jnp.where(valid & (other == jk // NORB), 1.0, 0.0),
                jnp.where(valid & (other == jk % NORB), 1.0, 0.0),
            ],
            axis=1,
        ).astype(BF)
        keep = jnp.where(keep == row, 1.0, 0.0)

        def fill(s, carry):
            for m in range(MODES):
                line = cm[pl.ds(m * SLOTS + s, 1), :]
                v[pl.ds(pl.multiple_of(s * (16 * MODES) + m * 16, 16), 16), :] = (
                    jnp.broadcast_to(line, (16, LANES)) * keep
                ).astype(BF)
            return carry

        lax.fori_loop(0, count, fill, 0)
        for part in range(SLOTS // 2):
            lo = part * 32 * MODES
            c12[lo : lo + 32 * MODES, :] = jnp.dot(
                v[lo : lo + 32 * MODES, :], spread, preferred_element_type=F32
            )

        def product(s, carry):
            for m in range(MODES):
                base = pl.multiple_of(s * (16 * MODES) + m * 16, 16)
                first = c12[pl.ds(base, 16), :LANES]
                second = c12[pl.ds(base, 16), LANES:]
                turns = [
                    second[0:8],
                    second[8:16],
                    pltpu.roll(second, 10, 0)[0:8],
                    pltpu.roll(second, 12, 0)[0:8],
                    pltpu.roll(second, 14, 0)[0:8],
                ]
                spreads = [jnp.broadcast_to(first[i : i + 1], (8, LANES)) for i in range(NORB)]
                rows = []
                for g in range(ROWS // 8):
                    lo = 8 * g // NORB
                    hi = min((8 * g + 7) // NORB, NORB - 1)
                    left = spreads[lo]
                    if hi != lo:
                        left = jnp.where(sub < NORB * hi - 8 * g, left, spreads[hi])
                    rows.append(left * turns[g % 5])
                t_ref[at + s, :, m * LANES : (m + 1) * LANES] = jnp.concatenate(rows, axis=0).astype(BF)
            return carry

        lax.fori_loop(0, count, product, 0)

    expand(col // NORB, ij % NORB, 0)
    expand(col % NORB, ij // NORB, SLOTS)

    odd = lax.axis_index("energy") % 2
    e_in = iota((2 * LANES, LANES), 0)
    e_out = iota((2 * LANES, LANES), 1)
    away = jnp.where(e_in < 128, e_in, jnp.where(e_in < 192, e_in - 192, e_in - 64)) - e_out
    for m in range(MODES):
        occ = occ_ref[m]
        step = off_ref[m]
        band = jnp.where(away == -step, occ, jnp.where(away == step, occ + 1.0, 0.0)).astype(BF)
        cols = slice(m * LANES, (m + 1) * LANES)
        s_ref[1 - odd, :, cols] = band
        s_ref[odd, 0:128, cols] = band[0:128]
        s_ref[odd, 128:192, cols] = band[192:256]
        s_ref[odd, 192:256, cols] = band[128:192]
    send.wait()


def shift_atom(center, halo, s_ref, which, lhs, low, store):
    lhs[0:ROWS, :LANES] = center[0:ROWS]
    lhs[0:ROWS, LANES:] = halo[0:ROWS]
    low[0:ROWS, :LANES] = center[96:SLAB].astype(F32)
    low[0:ROWS, LANES:] = halo[96:SLAB].astype(F32)
    low[ROWS:, :] = jnp.zeros((PITCH - ROWS, 256), F32)
    lhs[PITCH : PITCH + ROWS, :] = low[4 : 4 + ROWS, :].astype(BF)
    for t in range(MODES // 2):
        out = jnp.dot(lhs[...], s_ref[which, :, t * 256 : (t + 1) * 256], preferred_element_type=F32)
        for mm in range(2):
            for r in range(2):
                store(
                    2 * t + mm,
                    r,
                    out[r * PITCH : r * PITCH + ROWS, mm * LANES : (mm + 1) * LANES].astype(BF),
                )


def halo_of(first, second, x):
    pick = iota((SLAB, LANES), 1) // KMAX == 1 - lax.axis_index("atom") % 2
    a = first[x % 4]
    b = second[x % 4]
    return jnp.where(pick, a, b) if x < 4 else jnp.where(pick, b, a)


def store_in(x_ref, at):
    def store(m, r, value):
        x_ref[at, m * LANES : m * LANES + ROWS, r * LANES : (r + 1) * LANES] = value

    return store


def unfold(total, rows):
    rows[0:ROWS, :] = total[:, :LANES]
    rows[SQ : SQ + ROWS, :] = total[:, LANES:]
    return rows[0:SLAB, :]


class Lists:
    def __init__(self, source, held, sem):
        self.held = held
        self.copy = pltpu.make_async_copy(source, held, sem)
        self.copy.start()

    def ready(self):
        self.copy.wait()
        return self.held


def run_jobs(jobs_ref, kind, chunk, t_ref, x_ref, acc):
    count = jobs_ref[4 * LISTS + kind]

    def step(i, carry):
        for j in range(chunk):
            job = jobs_ref[kind * LISTS + i * chunk + j]
            t, src, dst = job & 63, (job >> 6) & 63, job >> 12
            acc[dst] = acc[dst] + jnp.dot(t_ref[t], x_ref[src], preferred_element_type=F32)
        return carry

    lax.fori_loop(0, (count + chunk - 1) // chunk, step, 0)


def rim_kernel(
    near, jobs_ref, g_ref, first, second, s_ref, t_ref, x_old, pay_ref, x, part, lhs, low, rows, held, sem
):
    lists = Lists(jobs_ref, held, sem)
    side = (near + lax.axis_index("atom")) % 2
    pick = iota((SLAB, LANES), 1) // KMAX == 1 - near
    for j in range(2):
        center = g_ref[6 * side + j]
        halo = jnp.where(pick, first[2 * side + j], second[2 * side + j])
        pay_ref[j] = center
        pay_ref[2 + j] = halo
        shift_atom(center, halo, s_ref, side, lhs.at[j], low.at[j], store_in(x, 6 * side + j))
    part[...] = jnp.zeros(part.shape, F32)
    run_jobs(lists.ready(), 1 + side, 4, t_ref, x, part)
    for j in range(2):
        pay_ref[4 + j] = unfold(part[j], rows.at[j]).astype(BF)


def local_kernel(
    jobs_ref, g_ref, first, second, s_ref, t_ref, x_old, inner_ref, rim_ref, x, acc, lhs, low, rows, held, sem
):
    lists = Lists(jobs_ref, held, sem)
    for at, atom in enumerate((2, 3, 4, 5)):
        halo = halo_of(first, second, atom)
        shift_atom(g_ref[atom], halo, s_ref, atom // 4, lhs.at[at], low.at[at], store_in(x, atom))
    acc[...] = jnp.zeros(acc.shape, F32)
    run_jobs(lists.ready(), 0, 8, t_ref, x, acc)
    for j in range(4):
        inner_ref[j] = unfold(acc[2 + j], rows.at[j]).astype(BF)
        rim_ref[j] = acc[j if j < 2 else j + 4]


def final_kernel(
    jobs_ref, cross_ref, near_ref, s_ref, t_ref, rim_ref, inner_ref, x_old, out_ref, x, acc, done, lhs, low, rows, held, sem, sems
):
    lists = Lists(jobs_ref, held, sem)
    odd = lax.axis_index("atom") % 2
    early = pltpu.make_async_copy(inner_ref, out_ref.at[2:6], sems.at[0])
    early.start()
    sides = ((1 - odd, near_ref), (odd, cross_ref))
    for n, (side, ref) in enumerate(sides):
        for j in range(2):
            at = 2 * n + j
            shift_atom(ref[j], ref[2 + j], s_ref, 1 - side, lhs.at[at], low.at[at], store_in(x, 2 * side + j))
    acc[0:4] = rim_ref[...]
    run_jobs(lists.ready(), 3, 4, t_ref, x, acc)
    copies = [early]
    for n, (side, ref) in enumerate(sides):
        for j in range(2):
            at = 2 * n + j
            done[at] = (unfold(acc[2 * side + j], rows.at[at]) + ref[4 + j].astype(F32)).astype(BF)
        copy = pltpu.make_async_copy(done.at[pl.ds(2 * n, 2)], out_ref.at[pl.ds(6 * side, 2)], sems.at[1 + n])
        copy.start()
        copies.append(copy)
    for copy in copies:
        copy.wait()


def swap(value, axis, start):
    count = lax.axis_size(axis)
    pairs = [(i, i + 1) for i in range(start, count - 1, 2)]
    return lax.ppermute(value, axis, pairs + [(b, a) for a, b in pairs])


def mixed_swap(value, start):
    parts, count = lax.axis_size("atom"), lax.axis_size("energy")
    pairs = []
    for part in range(parts):
        for i in range((start + part) % 2, count - 1, 2):
            pairs.append((part * count + i, part * count + i + 1))
    return lax.ppermute(value, ("atom", "energy"), pairs + [(b, a) for a, b in pairs])


def call(kernel, outs, scratch, flops, moved, specs, out_specs, aliases={}):
    return pl.pallas_call(
        kernel,
        out_shape=outs,
        in_specs=specs,
        out_specs=out_specs,
        scratch_shapes=scratch,
        input_output_aliases=aliases,
        compiler_params=pltpu.CompilerParams(vmem_limit_bytes=32 * 1024 * 1024),
        cost_estimate=pl.CostEstimate(flops=flops, bytes_accessed=moved, transcendentals=0),
    )


def per_device(green, coupling, pairs, counts, occupation, offsets):
    atoms, slab, e_dev = green.shape
    shape = jax.ShapeDtypeStruct
    dma = pltpu.SemaphoreType.DMA
    pairs = pairs.T

    half = shape((atoms // 2, slab, e_dev), BF)
    taken = (green, coupling, pairs, occupation, offsets)
    first, second, g, coup, pairs, occ, off = call(
        pack_kernel,
        (half, half) + tuple(shape(v.shape, v.dtype) for v in taken),
        [dma((5,))],
        int(1e6),
        int(1e6),
        [HBM] * 5,
        (VMEM,) * 7,
    )(*[pltpu.with_memory_space_constraint(v, pltpu.HBM) for v in taken])
    first = mixed_swap(first, 1)
    second = mixed_swap(second, 0)

    shifted = shape((ATOMS, DEPTH, 256), BF)
    t, s, jobs, x = call(
        build_kernel,
        (shape((2 * SLOTS, ROWS, DEPTH), BF), shape((2, 256, DEPTH), BF), shape((4 * LISTS + 4,), I32), shifted),
        [
            pltpu.VMEM((MODES * SLOTS, LANES), F32),
            pltpu.VMEM((MODES * SLOTS * 16, LANES), BF),
            pltpu.VMEM((MODES * SLOTS * 16, 256), F32),
            pltpu.SMEM((2, SLOTS), I32),
            pltpu.SMEM((MODES,), F32),
            pltpu.SMEM((MODES,), I32),
            pltpu.SMEM((4 * LISTS + 4,), I32),
            dma((4,)),
        ],
        int(3e9),
        int(8e6),
        [SMEM] + [VMEM] * 4,
        (VMEM,) * 4,
    )(counts, pairs, occ, off, coup)

    spare = [
        pltpu.VMEM((4, 2 * PITCH, 256), BF),
        pltpu.VMEM((4, PITCH, 256), F32),
        pltpu.VMEM((4, 208, LANES), F32),
        pltpu.SMEM((4 * LISTS + 4,), I32),
        dma(()),
    ]
    payload = shape((6, slab, e_dev), BF)
    swapped = []
    for near in range(2):
        pay, x = call(
            functools.partial(rim_kernel, near),
            (payload, shifted),
            [pltpu.VMEM((3, ROWS, 256), F32)] + spare,
            int(5e8),
            int(1e6),
            [VMEM] * 7,
            (VMEM, VMEM),
            {6: 1},
        )(jobs, g, first, second, s, t, x)
        swapped.append(swap(pay, "atom", 1 - near))
    cross, near = swapped
    inner, rim, x = call(
        local_kernel,
        (shape((4, slab, e_dev), BF), shape((4, ROWS, 256), F32), shifted),
        [pltpu.VMEM((9, ROWS, 256), F32)] + spare,
        int(3e9),
        int(1e6),
        [VMEM] * 7,
        (VMEM,) * 3,
        {6: 2},
    )(jobs, g, first, second, s, t, x)

    return call(
        final_kernel,
        (shape((atoms, slab, e_dev), BF), shifted),
        [pltpu.VMEM((5, ROWS, 256), F32), pltpu.VMEM((4, slab, e_dev), BF)] + spare + [dma((3,))],
        int(1e9),
        int(1e6),
        [VMEM] * 8,
        (HBM, VMEM),
        {7: 1},
    )(jobs, cross, near, s, t, rim, inner, x)[0]


def solution(mesh):
    placed = (P("atom", None, "energy"), P("atom", None), P("atom", None), P("atom"), P(), P())
    return jax.shard_map(
        per_device, mesh=mesh, in_specs=placed, out_specs=P("atom", None, "energy"), check_vma=False
    )
```

```python
import functools

import jax
import jax.numpy as jnp
from jax import lax
from jax.experimental import pallas as pl
from jax.experimental.pallas import tpu as pltpu
from jax.sharding import PartitionSpec as P

NORB = 10
MODES = 8
KMAX = 64
SQ = NORB * NORB
ROWS = 104
PITCH = 112
LANES = 128
DEPTH = MODES * LANES
SLOTS = 16
ATOMS = 8
SLAB = 2 * SQ
LISTS = 48
BF = jnp.bfloat16
F32 = jnp.float32
I32 = jnp.int32
VMEM = pl.BlockSpec(memory_space=pltpu.VMEM)
SMEM = pl.BlockSpec(memory_space=pltpu.SMEM)
HBM = pl.BlockSpec(memory_space=pltpu.HBM)


def iota(shape, dim):
    return lax.broadcasted_iota(I32, shape, dim)


def pack_kernel(g_hbm, coup_hbm, pairs_hbm, occ_hbm, off_hbm, first, second, g, coup, pairs, occ, off, sems):
    half = ATOMS // 2
    moves = ((g_hbm, g), (coup_hbm, coup), (pairs_hbm, pairs), (occ_hbm, occ), (off_hbm, off))
    copies = [pltpu.make_async_copy(src, dst, sems.at[i]) for i, (src, dst) in enumerate(moves)]
    for copy in copies:
        copy.start()
    odd = lax.axis_index("energy") % 2
    pick = (iota((SLAB, LANES), 1) // KMAX) == (odd + 1 + lax.axis_index("atom")) % 2
    copies[0].wait()
    for x in range(half):
        turned = pltpu.roll(g[x + half * odd].astype(F32), KMAX, 1).astype(BF)
        kept = g[x + half - half * odd]
        first[x] = jnp.where(pick, turned, kept)
        second[x] = jnp.where(pick, kept, turned)
    for copy in copies[1:]:
        copy.wait()


def build_kernel(
    cnt_ref, pairs_in, occ_in, off_in, coup_ref, t_ref, s_ref, jobs_out, x_ref, cm, v, c12, pairs_ref, occ_ref, off_ref, jobs_ref, sems
):
    moves = ((pairs_in, pairs_ref), (occ_in, occ_ref), (off_in, off_ref))
    copies = [pltpu.make_async_copy(src, dst, sems.at[i]) for i, (src, dst) in enumerate(moves)]
    for copy in copies:
        copy.start()
    count = cnt_ref[0]
    base = lax.axis_index("atom") * ATOMS
    for x in range(ATOMS):
        for m in range(MODES):
            x_ref[x, m * LANES + 96 : (m + 1) * LANES, :] = jnp.zeros((32, 256), BF)

    def listed(s, carry):
        near, down, up, far = carry
        first = pairs_ref[0, s] - base
        second = pairs_ref[1, s] - base
        local = jnp.where((second >= 0) & (second < ATOMS), 1, 0)
        below = jnp.where(second < 0, 1, 0)
        above = 1 - local - below
        jobs_ref[near] = s + 64 * second + 4096 * first
        jobs_ref[near + 1] = s + SLOTS + 64 * first + 4096 * second
        jobs_ref[LISTS + down] = s + SLOTS + 64 * first + 4096 * (second + 2)
        jobs_ref[2 * LISTS + up] = s + SLOTS + 64 * first + 4096 * (second - ATOMS)
        jobs_ref[3 * LISTS + far] = s + 64 * (second + 2 - 8 * above) + 4096 * (first - 4 * above)
        return near + 2 * local, down + below, up + above, far + 1 - local

    for copy in copies:
        copy.wait()
    counted = lax.fori_loop(0, count, listed, (jnp.int32(0),) * 4)
    for kind, (many, spare) in enumerate(zip(counted, (ATOMS, 2, 2, 4))):
        for j in range(8):
            jobs_ref[kind * LISTS + many + j] = 4096 * spare
        jobs_ref[4 * LISTS + kind] = many
    send = pltpu.make_async_copy(jobs_ref, jobs_out, sems.at[3])
    send.start()

    coup = coup_ref[...].astype(F32)
    width = 7 * LANES
    coup = jnp.concatenate([coup, jnp.zeros((SLOTS, width - MODES * SQ), F32)], axis=1)
    lane = iota((SLOTS, LANES), 1)
    for m in range(MODES):
        part = coup if m == 0 else pltpu.roll(coup, width - m * SQ, 1)
        cm[m * SLOTS : (m + 1) * SLOTS, :] = jnp.where(lane < SQ, part[:, :LANES], 0.0)

    ij = iota((LANES, LANES), 0)
    jk = iota((LANES, LANES), 1)
    valid = (ij < SQ) & (jk < SQ)
    row = iota((16, LANES), 0) % NORB
    col = iota((16, LANES), 1)
    sub = iota((8, LANES), 0)

    def expand(keep, other, at):
        spread = jnp.concatenate(
            [
                jnp.where(valid & (other == jk // NORB), 1.0, 0.0),
                jnp.where(valid & (other == jk % NORB), 1.0, 0.0),
            ],
            axis=1,
        ).astype(BF)
        keep = jnp.where(keep == row, 1.0, 0.0)

        def fill(i, carry):
            for s, m in ((s, m) for s in (2 * i, 2 * i + 1) for m in range(MODES)):
                line = cm[pl.ds(m * SLOTS + s, 1), :]
                v[pl.ds(pl.multiple_of(s * (16 * MODES) + m * 16, 16), 16), :] = (
                    jnp.broadcast_to(line, (16, LANES)) * keep
                ).astype(BF)
            return carry

        lax.fori_loop(0, (count + 1) // 2, fill, 0)
        for part in range(SLOTS // 2):
            lo = part * 32 * MODES
            c12[lo : lo + 32 * MODES, :] = jnp.dot(
                v[lo : lo + 32 * MODES, :], spread, preferred_element_type=F32
            )

        def product(i, carry):
            for s, m in ((s, m) for s in (2 * i, 2 * i + 1) for m in range(MODES)):
                base = pl.multiple_of(s * (16 * MODES) + m * 16, 16)
                first = c12[pl.ds(base, 16), :LANES]
                second = c12[pl.ds(base, 16), LANES:]
                turns = [
                    second[0:8],
                    second[8:16],
                    pltpu.roll(second, 10, 0)[0:8],
                    pltpu.roll(second, 12, 0)[0:8],
                    pltpu.roll(second, 14, 0)[0:8],
                ]
                spreads = [jnp.broadcast_to(first[i : i + 1], (8, LANES)) for i in range(NORB)]
                rows = []
                for g in range(ROWS // 8):
                    lo = 8 * g // NORB
                    hi = min((8 * g + 7) // NORB, NORB - 1)
                    left = spreads[lo]
                    if hi != lo:
                        left = jnp.where(sub < NORB * hi - 8 * g, left, spreads[hi])
                    rows.append(left * turns[g % 5])
                t_ref[at + s, :, m * LANES : (m + 1) * LANES] = jnp.concatenate(rows, axis=0).astype(BF)
            return carry

        lax.fori_loop(0, (count + 1) // 2, product, 0)

    expand(col // NORB, ij % NORB, 0)
    expand(col % NORB, ij // NORB, SLOTS)

    odd = lax.axis_index("energy") % 2
    e_in = iota((2 * LANES, LANES), 0)
    e_out = iota((2 * LANES, LANES), 1)
    away = jnp.where(e_in < 128, e_in, jnp.where(e_in < 192, e_in - 192, e_in - 64)) - e_out
    for m in range(MODES):
        occ = occ_ref[m]
        step = off_ref[m]
        band = jnp.where(away == -step, occ, jnp.where(away == step, occ + 1.0, 0.0)).astype(BF)
        cols = slice(m * LANES, (m + 1) * LANES)
        s_ref[1 - odd, :, cols] = band
        s_ref[odd, 0:128, cols] = band[0:128]
        s_ref[odd, 128:192, cols] = band[192:256]
        s_ref[odd, 192:256, cols] = band[128:192]
    send.wait()


def shift_atom(center, halo, s_ref, which, lhs, low, store):
    lhs[0:ROWS, :LANES] = center[0:ROWS]
    lhs[0:ROWS, LANES:] = halo[0:ROWS]
    low[0:ROWS, :LANES] = center[96:SLAB].astype(F32)
    low[0:ROWS, LANES:] = halo[96:SLAB].astype(F32)
    low[ROWS:, :] = jnp.zeros((PITCH - ROWS, 256), F32)
    lhs[PITCH : PITCH + ROWS, :] = low[4 : 4 + ROWS, :].astype(BF)
    for t in range(MODES // 2):
        out = jnp.dot(lhs[...], s_ref[which, :, t * 256 : (t + 1) * 256], preferred_element_type=F32)
        for mm in range(2):
            for r in range(2):
                store(
                    2 * t + mm,
                    r,
                    out[r * PITCH : r * PITCH + ROWS, mm * LANES : (mm + 1) * LANES].astype(BF),
                )


def halo_of(first, second, x):
    pick = iota((SLAB, LANES), 1) // KMAX == 1 - lax.axis_index("atom") % 2
    a = first[x % 4]
    b = second[x % 4]
    return jnp.where(pick, a, b) if x < 4 else jnp.where(pick, b, a)


def store_in(x_ref, at):
    def store(m, r, value):
        x_ref[at, m * LANES : m * LANES + ROWS, r * LANES : (r + 1) * LANES] = value

    return store


def unfold(total, rows):
    rows[0:ROWS, :] = total[:, :LANES]
    rows[SQ : SQ + ROWS, :] = total[:, LANES:]
    return rows[0:SLAB, :]


class Lists:
    def __init__(self, source, held, sem):
        self.held = held
        self.copy = pltpu.make_async_copy(source, held, sem)
        self.copy.start()

    def ready(self):
        self.copy.wait()
        return self.held


def run_jobs(jobs_ref, kind, chunk, t_ref, x_ref, acc):
    count = jobs_ref[4 * LISTS + kind]

    def step(i, carry):
        for j in range(chunk):
            job = jobs_ref[kind * LISTS + i * chunk + j]
            t, src, dst = job & 63, (job >> 6) & 63, job >> 12
            acc[dst] = acc[dst] + jnp.dot(t_ref[t], x_ref[src], preferred_element_type=F32)
        return carry

    lax.fori_loop(0, (count + chunk - 1) // chunk, step, 0)


def rim_kernel(
    near, jobs_ref, g_ref, first, second, s_ref, t_ref, x_old, pay_ref, x, part, lhs, low, rows, held, sem
):
    lists = Lists(jobs_ref, held, sem)
    side = (near + lax.axis_index("atom")) % 2
    pick = iota((SLAB, LANES), 1) // KMAX == 1 - near
    for j in range(2):
        center = g_ref[6 * side + j]
        halo = jnp.where(pick, first[2 * side + j], second[2 * side + j])
        pay_ref[j] = center
        pay_ref[2 + j] = halo
        shift_atom(center, halo, s_ref, side, lhs.at[j], low.at[j], store_in(x, 6 * side + j))
    part[...] = jnp.zeros(part.shape, F32)
    run_jobs(lists.ready(), 1 + side, 4, t_ref, x, part)
    for j in range(2):
        pay_ref[4 + j] = unfold(part[j], rows.at[j]).astype(BF)


def local_kernel(
    jobs_ref, g_ref, first, second, s_ref, t_ref, x_old, inner_ref, rim_ref, x, acc, lhs, low, rows, held, sem
):
    lists = Lists(jobs_ref, held, sem)
    for at, atom in enumerate((2, 3, 4, 5)):
        halo = halo_of(first, second, atom)
        shift_atom(g_ref[atom], halo, s_ref, atom // 4, lhs.at[at], low.at[at], store_in(x, atom))
    acc[...] = jnp.zeros(acc.shape, F32)
    run_jobs(lists.ready(), 0, 8, t_ref, x, acc)
    for j in range(4):
        inner_ref[j] = unfold(acc[2 + j], rows.at[j]).astype(BF)
        rim_ref[j] = acc[j if j < 2 else j + 4]


def final_kernel(
    jobs_ref, cross_ref, near_ref, s_ref, t_ref, rim_ref, inner_ref, x_old, out_ref, x, acc, done, lhs, low, rows, held, sem, sems
):
    lists = Lists(jobs_ref, held, sem)
    odd = lax.axis_index("atom") % 2
    early = pltpu.make_async_copy(inner_ref, out_ref.at[2:6], sems.at[0])
    early.start()
    sides = ((1 - odd, near_ref), (odd, cross_ref))
    for n, (side, ref) in enumerate(sides):
        for j in range(2):
            at = 2 * n + j
            shift_atom(ref[j], ref[2 + j], s_ref, 1 - side, lhs.at[at], low.at[at], store_in(x, 2 * side + j))
    acc[0:4] = rim_ref[...]
    run_jobs(lists.ready(), 3, 4, t_ref, x, acc)
    copies = [early]
    for n, (side, ref) in enumerate(sides):
        for j in range(2):
            at = 2 * n + j
            done[at] = (unfold(acc[2 * side + j], rows.at[at]) + ref[4 + j].astype(F32)).astype(BF)
        copy = pltpu.make_async_copy(done.at[pl.ds(2 * n, 2)], out_ref.at[pl.ds(6 * side, 2)], sems.at[1 + n])
        copy.start()
        copies.append(copy)
    for copy in copies:
        copy.wait()


def swap(value, axis, start):
    count = lax.axis_size(axis)
    pairs = [(i, i + 1) for i in range(start, count - 1, 2)]
    return lax.ppermute(value, axis, pairs + [(b, a) for a, b in pairs])


def mixed_swap(value, start):
    parts, count = lax.axis_size("atom"), lax.axis_size("energy")
    pairs = []
    for part in range(parts):
        for i in range((start + part) % 2, count - 1, 2):
            pairs.append((part * count + i, part * count + i + 1))
    return lax.ppermute(value, ("atom", "energy"), pairs + [(b, a) for a, b in pairs])


def call(kernel, outs, scratch, flops, moved, specs, out_specs, aliases={}):
    return pl.pallas_call(
        kernel,
        out_shape=outs,
        in_specs=specs,
        out_specs=out_specs,
        scratch_shapes=scratch,
        input_output_aliases=aliases,
        compiler_params=pltpu.CompilerParams(vmem_limit_bytes=32 * 1024 * 1024),
        cost_estimate=pl.CostEstimate(flops=flops, bytes_accessed=moved, transcendentals=0),
    )


def per_device(green, coupling, pairs, counts, occupation, offsets):
    atoms, slab, e_dev = green.shape
    shape = jax.ShapeDtypeStruct
    dma = pltpu.SemaphoreType.DMA
    pairs = pairs.T

    half = shape((atoms // 2, slab, e_dev), BF)
    taken = (green, coupling, pairs, occupation, offsets)
    first, second, g, coup, pairs, occ, off = call(
        pack_kernel,
        (half, half) + tuple(shape(v.shape, v.dtype) for v in taken),
        [dma((5,))],
        int(1e6),
        int(1e6),
        [HBM] * 5,
        (VMEM,) * 7,
    )(*[pltpu.with_memory_space_constraint(v, pltpu.HBM) for v in taken])
    first = mixed_swap(first, 1)
    second = mixed_swap(second, 0)

    shifted = shape((ATOMS, DEPTH, 256), BF)
    t, s, jobs, x = call(
        build_kernel,
        (shape((2 * SLOTS, ROWS, DEPTH), BF), shape((2, 256, DEPTH), BF), shape((4 * LISTS + 4,), I32), shifted),
        [
            pltpu.VMEM((MODES * SLOTS, LANES), F32),
            pltpu.VMEM((MODES * SLOTS * 16, LANES), BF),
            pltpu.VMEM((MODES * SLOTS * 16, 256), F32),
            pltpu.SMEM((2, SLOTS), I32),
            pltpu.SMEM((MODES,), F32),
            pltpu.SMEM((MODES,), I32),
            pltpu.SMEM((4 * LISTS + 4,), I32),
            dma((4,)),
        ],
        int(3e9),
        int(8e6),
        [SMEM] + [VMEM] * 4,
        (VMEM,) * 4,
    )(counts, pairs, occ, off, coup)

    spare = [
        pltpu.VMEM((4, 2 * PITCH, 256), BF),
        pltpu.VMEM((4, PITCH, 256), F32),
        pltpu.VMEM((4, 208, LANES), F32),
        pltpu.SMEM((4 * LISTS + 4,), I32),
        dma(()),
    ]
    payload = shape((6, slab, e_dev), BF)
    swapped = []
    for near in range(2):
        pay, x = call(
            functools.partial(rim_kernel, near),
            (payload, shifted),
            [pltpu.VMEM((3, ROWS, 256), F32)] + spare,
            int(5e8),
            int(1e6),
            [VMEM] * 7,
            (VMEM, VMEM),
            {6: 1},
        )(jobs, g, first, second, s, t, x)
        swapped.append(swap(pay, "atom", 1 - near))
    cross, near = swapped
    inner, rim, x = call(
        local_kernel,
        (shape((4, slab, e_dev), BF), shape((4, ROWS, 256), F32), shifted),
        [pltpu.VMEM((9, ROWS, 256), F32)] + spare,
        int(3e9),
        int(1e6),
        [VMEM] * 7,
        (VMEM,) * 3,
        {6: 2},
    )(jobs, g, first, second, s, t, x)

    return call(
        final_kernel,
        (shape((atoms, slab, e_dev), BF), shifted),
        [pltpu.VMEM((5, ROWS, 256), F32), pltpu.VMEM((4, slab, e_dev), BF)] + spare + [dma((3,))],
        int(1e9),
        int(1e6),
        [VMEM] * 8,
        (HBM, VMEM),
        {7: 1},
    )(jobs, cross, near, s, t, rim, inner, x)[0]


def solution(mesh):
    placed = (P("atom", None, "energy"), P("atom", None), P("atom", None), P("atom"), P(), P())
    return jax.shard_map(
        per_device, mesh=mesh, in_specs=placed, out_specs=P("atom", None, "energy"), check_vma=False
    )
```
